256 devices in a mesh: dom: 32 (over y, z_hi, core), rep: 8 (over x, z_lo).
Axes of the slice: x: 4, y: 4, z: 8 (z_hi: 4, z_lo: 2; z = z_hi * 2 + z_lo), core: 2. Of those that a mesh axis runs over, the one named last changes fastest.
Arguments:
- features: bfloat16 [16384, 768], P('dom'), may hold values from -6 to 6
- tiles: bfloat16 [128, 32, 4, 128, 128], P('dom', 'rep'), may hold values from -0.046875 to 0.046875
- tile_cols: int32 [128, 32, 4], P('dom', 'rep'), may hold values from 0 to 3
- tile_mask: int32 [128, 32, 4], P('dom', 'rep'), may hold values from 0 to 1, as said below
- weight: bfloat16 [768, 768], replicated, may hold values from -0.21875 to 0.21875
- bias: float32 [768], replicated, may hold values from -3 to 3
- cotangent: bfloat16 [16384, 768], P(('dom', 'rep')), may hold values from -0.046875 to 0.046875
Outputs:
- output: bfloat16 [16384, 768], P(('dom', 'rep'))
- grad_weight: float32 [768, 768], replicated
- grad_bias: float32 [768], replicated
The draws below stay inside these ranges and needn't reach their ends.
Inputs may be any that keep to these rules, and one draw needn't show every extreme that they name: `tile_mask`: for each row block and source, the live slots come first and slot 0 is always live.
All inputs are finite; a program needn't handle non-finite values.
Results may differ from the reference program's by a relative error of at most 0.02.
Values may be sent and summed in bfloat16 or wider, within the bound.
No kernel may reach another device: no remote copies, remote signals or barrier semaphores. Data moves between devices by JAX's collectives and lax.ppermute only.
A program may use at most 128 MiB of HBM per device.

```python
import jax
import jax.numpy as jnp
from jax import lax

D = 768
TB = 128
RB = 4
K = 4
NBLK = 128
NODES = 16384
N_DOM = 32
N_REP = 8


def draw_tile_mask(key, part):
    key = jax.random.fold_in(key, 7)
    counts = jax.random.randint(key, (NBLK, N_DOM, 1), 1, K + 1)
    slots = jnp.arange(K).astype(jnp.int32)
    return (slots[None, None, :] < counts).astype(jnp.int32)


def touch_ends(array, own_key, smallest, high):
    longest = array.shape.index(max(array.shape))
    spots = []
    for shift in (0, 1):
        where = [jax.random.randint(jax.random.fold_in(own_key, axis), (), 0, length) for axis, length in enumerate(array.shape)]
        where[longest] = (where[longest] + shift) % array.shape[longest]
        spots.append(tuple(where))
    return array.at[spots[0]].set(smallest).at[spots[1]].set(high)


def block_scale(rng, extent, shards, smallest, high):
    factor_of, own = 1.0, jax.random.fold_in(rng, 6)
    for axis_at, blocks in shards:
        draws = jnp.exp(jax.random.uniform(jax.random.fold_in(own, axis_at), (blocks,), jnp.float32, smallest / len(shards), high / len(shards)))
        factor_of = factor_of * jnp.repeat(draws, extent[axis_at] // blocks).reshape([-1 if axis == axis_at else 1 for axis in range(len(extent))])
    return factor_of


def normal_values(stream_key, shape, width, bound, cuts=(), dtype=jnp.bfloat16):
    factor_of = block_scale(stream_key, shape, cuts, -0.22, 0.18) if cuts else 1.0
    array = jax.random.normal(stream_key, shape, jnp.float32) * width * factor_of
    return jnp.minimum(jnp.maximum(array, -bound), bound).astype(dtype)


def setup_inputs(seed: int = 0) -> dict:
    key_of = jax.random.split(jax.random.key(seed), 8)
    features = normal_values(key_of[0], (NODES, D), 1.0, 6.0, ((0, 32),))
    tiles = normal_values(key_of[1], (NBLK, N_DOM, K, TB, TB), (N_DOM * K * TB) ** -0.5, 0.046875, ((0, 32), (1, 8)))
    tile_cols = touch_ends(jax.random.randint(key_of[2], (NBLK, N_DOM, K), 0, RB), jax.random.fold_in(key_of[2], 1), 0, RB - 1).astype(jnp.int32)
    tile_mask = draw_tile_mask(jax.random.fold_in(key_of[7], 71), 0)
    weight = normal_values(key_of[4], (D, D), D ** -0.5, 0.21875)
    bias = normal_values(key_of[5], (D,), 0.5, 3.0, (), jnp.float32)
    cotangent = normal_values(key_of[6], (NODES, D), (1.0 / (RB * TB * N_DOM) ** 0.5), 0.046875, ((0, 256),))
    return dict(features=features, tiles=tiles, tile_cols=tile_cols, tile_mask=tile_mask, weight=weight, bias=bias, cotangent=cotangent)


def reference(features, tiles, tile_cols, tile_mask, weight, bias, cotangent):
    blocks = features.reshape(NBLK, TB, D)
    offsets = (jnp.arange(N_DOM) * RB).astype(jnp.int32)

    def aggregate_block(packed):
        tile_set, columns, live = packed
        global_cols = (offsets[:, None] + columns).astype(jnp.int32)
        picked = blocks[global_cols].astype(jnp.float32)
        masked = tile_set.astype(jnp.float32) * live[:, :, None, None].astype(jnp.float32)
        per_source = jnp.einsum("skij,skjd->sid", masked, picked)
        grouped = jnp.sum(per_source.reshape(N_REP, N_DOM // N_REP, TB, D), axis=1)
        rounded = lax.optimization_barrier(grouped.astype(jnp.bfloat16))
        return jnp.sum(rounded.astype(jnp.float32), axis=0)

    aggregate = lax.map(aggregate_block, (tiles, tile_cols, tile_mask)).reshape(NODES, D)
    mixed = aggregate.astype(jnp.bfloat16)
    pre_act = jnp.dot(mixed, weight, preferred_element_type=jnp.float32) + bias
    output = (pre_act * jax.nn.sigmoid(pre_act)).astype(jnp.bfloat16)
    sigmoid_pre = jax.nn.sigmoid(pre_act)
    grad_pre = cotangent.astype(jnp.float32) * sigmoid_pre * (1.0 + pre_act * (1.0 - sigmoid_pre))
    grad_low = grad_pre.astype(jnp.bfloat16)
    grad_weight = jnp.dot(mixed.T, grad_low, preferred_element_type=jnp.float32)
    grad_bias = jnp.sum(grad_pre, axis=0)
    return output, grad_weight, grad_bias
```

```python
import jax
import jax.numpy as jnp
import numpy as np
from jax import lax
from jax.experimental import pallas as pl
from jax.experimental.pallas import tpu as pltpu
from jax.sharding import Mesh, PartitionSpec as P

AXES = ("y", "zh", "core", "x", "zl")
SIZES = (4, 4, 2, 4, 2)
DOM = ("y", "zh", "core")
REP = ("x", "zl")
PLANE = ("x", "y")
ZAXIS = ("zh", "zl")
BF = jnp.bfloat16
F32 = jnp.float32
VMEM_LIMIT = 48 * 1024 * 1024


def vmem():
    return pl.BlockSpec(memory_space=pltpu.VMEM)


def smem():
    return pl.BlockSpec(memory_space=pltpu.SMEM)


def anyspace():
    return pl.BlockSpec(memory_space=pl.ANY)


def params():
    return pltpu.CompilerParams(vmem_limit_bytes=VMEM_LIMIT)


def shift(n, k):
    return [(i, (i + k) % n) for i in range(n)]


def first_hop():
    pairs = []
    for target in range(int(np.prod(SIZES))):
        y, zh, core, x, zl = (int(v) for v in np.unravel_index(target, SIZES))
        source = (x, 2 * zl + y // 2, y % 2, (x + zh) % 4, core)
        pairs.append((int(np.ravel_multi_index(source, SIZES)), target))
    return sorted(pairs)


def aggregate_kernel(place, cols, live, tiles, *rest):
    parts, out, feat, sems = rest[:8], rest[8], rest[9], rest[10]
    copies = [
        pltpu.make_async_copy(part, feat.at[pl.ds(i * 256, 256)], sems.at[i])
        for i, part in enumerate(parts)
    ]
    for copy in copies:
        copy.start()
    for copy in copies:
        copy.wait()
    y, core = place[0], place[1]
    for b in range(4):
        total = jnp.zeros((128, 768), F32)
        for s in range(4):
            back = lax.rem(y - s + 4, 4)
            for pair in range(2):
                lhs, rhs = [], []
                for k in (2 * pair, 2 * pair + 1):
                    c = cols[b, s, k]
                    half = c // 2
                    away = lax.rem(half + core, 2)
                    row = (2 * back + away) * 256 + lax.rem(c, 2) * 128
                    rhs.append(feat[pl.ds(pl.multiple_of(row, 128), 128), :])
                    tile = tiles[b, s, k]
                    lhs.append(jnp.where(live[b, s, k] != 0, tile, jnp.zeros_like(tile)))
                total = total + jnp.dot(
                    jnp.concatenate(lhs, axis=1),
                    jnp.concatenate(rhs, axis=0),
                    preferred_element_type=F32,
                )
        out[pl.ds(b * 128, 128), :] = total.astype(BF)


def layer_kernel(recv, weight, bias, cot, out, packed):
    total = recv[0].astype(F32)
    for r in range(1, 8):
        total = total + recv[r].astype(F32)
    mixed = total.astype(BF)
    pre = jnp.dot(mixed, weight[...], preferred_element_type=F32) + bias[...]
    sig = jax.nn.sigmoid(pre)
    out[...] = (pre * sig).astype(BF)
    grad = cot[...].astype(F32) * sig * (1.0 + pre * (1.0 - sig))
    low = grad.astype(BF).astype(F32)
    wide = mixed.astype(F32)
    for i in range(4):
        left = wide[:, i * 192 : (i + 1) * 192]
        for j in range(4):
            both = jnp.concatenate([left, low[:, j * 192 : (j + 1) * 192]], axis=1)
            packed[i * 4 + j] = both.astype(BF)


def with_bias(block, row):
    high = row.astype(BF).astype(F32)
    low = row - high
    at = lax.broadcasted_iota(jnp.int32, (16, 384), 0)
    extra = jnp.where(at == 0, high, jnp.where(at == 1, low, 0.0))
    return jnp.concatenate([block, extra], axis=0)


def block_kernel(place, recv, keep, send):
    data = recv[...]
    left = data[:, :192]
    right = data[:, 192:]
    block = lax.dot_general(left, right, (((0,), (0,)), ((), ())), preferred_element_type=F32)
    row = jnp.sum(right.astype(F32), axis=0, keepdims=True)
    row = jnp.concatenate([row, row], axis=1)
    halves = [
        with_bias(
            jnp.concatenate([block[h * 96 : h * 96 + 48], block[h * 96 + 48 : h * 96 + 96]], axis=1),
            row,
        )
        for h in range(2)
    ]
    core = place[1]
    keep[...] = jnp.where(core == 0, halves[0], halves[1])
    send[...] = jnp.where(core == 0, halves[1], halves[0]).astype(BF)


def resplit(total):
    row = total[48:49] + total[49:50]
    return with_bias(total[:48], row).astype(BF)


def pair_kernel(copies, keep, recv, out):
    value = resplit(keep[...] + recv[...].astype(F32))
    for i in range(copies):
        out[i] = value


def sum_kernel(copies, recv, out):
    total = recv[0].astype(F32)
    for r in range(1, 8):
        total = total + recv[r].astype(F32)
    value = resplit(total)
    for i in range(copies):
        out[i] = value


def final_kernel(place, own, other, grad, bias):
    core = place[1]
    for source, at in ((own, core), (other, 1 - core)):
        for i in range(4):
            pieces = [source[i * 4 + j].astype(F32) for j in range(4)]
            for h in range(2):
                rows = jnp.concatenate(
                    [piece[:48, h * 192 : (h + 1) * 192] for piece in pieces], axis=1
                )
                start = pl.multiple_of(i * 192 + at * 96 + h * 48, 16)
                grad[pl.ds(start, 48), :] = rows
    bias[...] = jnp.concatenate(
        [
            own[j, 48:64, :].astype(F32)[0:1, :192] + own[j, 48:64, :].astype(F32)[1:2, :192]
            for j in range(4)
        ],
        axis=1,
    )


def call(kernel, shapes, specs, out_specs, scratch=()):
    return pl.pallas_call(
        kernel,
        out_shape=shapes,
        in_specs=specs,
        out_specs=out_specs,
        scratch_shapes=scratch,
        compiler_params=params(),
    )


def struct(shape, dtype):
    return jax.ShapeDtypeStruct(shape, dtype)


def on_device(features, tiles, tile_cols, tile_mask, weight, bias, cotangent):
    place = jnp.stack([lax.axis_index("y"), lax.axis_index("core")]).astype(jnp.int32)
    with jax.named_scope("spread_features"):
        half = lax.dynamic_slice_in_dim(features, lax.axis_index("zl") * 256, 256, 0)
        own = lax.ppermute(half, AXES, first_hop())
        parts = [own] + [lax.ppermute(own, "y", shift(4, k)) for k in (1, 2, 3)]
        swapped = [lax.ppermute(part, "core", shift(2, 1)) for part in parts]
        blocks = [block for pair in zip(parts, swapped) for block in pair]
    with jax.named_scope("aggregate"):
        partial = call(
            aggregate_kernel,
            struct((512, 768), BF),
            [smem(), smem(), smem(), vmem()] + [anyspace()] * 8,
            vmem(),
            [pltpu.VMEM((2048, 768), BF), pltpu.SemaphoreType.DMA((8,))],
        )(place, tile_cols, tile_mask, tiles, *blocks)
    with jax.named_scope("sum_over_rep"):
        recv = lax.all_to_all(partial, REP, 0, 0, tiled=True).reshape(8, 64, 768)
    with jax.named_scope("layer"):
        output, packed = call(
            layer_kernel,
            (struct((64, 768), BF), struct((16, 64, 384), BF)),
            [vmem()] * 4,
            (vmem(), vmem()),
        )(recv, weight, bias.reshape(1, 768), cotangent)
    with jax.named_scope("exchange_rows"):
        rows = lax.all_to_all(packed.reshape(1024, 384), PLANE, 0, 0, tiled=True)
    with jax.named_scope("weight_block"):
        keep, send = call(
            block_kernel,
            (struct((64, 384), F32), struct((64, 384), BF)),
            [smem(), vmem()],
            (vmem(), vmem()),
        )(place, rows)
        other = lax.ppermute(send, "core", shift(2, 1))
        pair = call(
            lambda *refs: pair_kernel(8, *refs),
            struct((8, 64, 384), BF),
            [vmem()] * 2,
            vmem(),
        )(keep, other)
    with jax.named_scope("sum_over_z"):
        chain = lax.all_to_all(pair.reshape(512, 384), ZAXIS, 0, 0, tiled=True)
        whole = call(
            lambda *refs: sum_kernel(16, *refs),
            struct((16, 64, 384), BF),
            [vmem()],
            vmem(),
        )(chain.reshape(8, 64, 384))
    with jax.named_scope("gather_plane"):
        mine = lax.all_to_all(whole.reshape(1024, 384), PLANE, 0, 0, tiled=True)
        theirs = lax.ppermute(mine, "core", shift(2, 1))
    with jax.named_scope("finish"):
        grad_weight, grad_bias = call(
            final_kernel,
            (struct((768, 768), F32), struct((1, 768), F32)),
            [smem(), vmem(), vmem()],
            (vmem(), vmem()),
        )(place, mine.reshape(16, 64, 384), theirs.reshape(16, 64, 384))
    return output, grad_weight, grad_bias.reshape(768)


def solution(mesh):
    fine = Mesh(mesh.devices.reshape(SIZES), AXES)
    placed = (
        P(DOM, None),
        P(DOM, REP, None, None, None),
        P(DOM, REP, None),
        P(DOM, REP, None),
        P(),
        P(),
        P(DOM + REP, None),
    )
    return jax.shard_map(
        on_device,
        mesh=fine,
        in_specs=placed,
        out_specs=(P(DOM + REP, None), P(), P()),
        check_vma=False,
    )
```

```python
import jax
import jax.numpy as jnp
import numpy as np
from jax import lax
from jax.experimental import pallas as pl
from jax.experimental.pallas import tpu as pltpu
from jax.sharding import Mesh, PartitionSpec as P

AXES = ("y", "zh", "core", "x", "zl")
SIZES = (4, 4, 2, 4, 2)
DOM = ("y", "zh", "core")
REP = ("x", "zl")
PLANE = ("x", "y")
ZAXIS = ("zh", "zl")
BF = jnp.bfloat16
F32 = jnp.float32
BACK = (0, 1, 3, 2)
VMEM_LIMIT = 48 * 1024 * 1024


def vmem():
    return pl.BlockSpec(memory_space=pltpu.VMEM)


def smem():
    return pl.BlockSpec(memory_space=pltpu.SMEM)


def anyspace():
    return pl.BlockSpec(memory_space=pl.ANY)


def params():
    return pltpu.CompilerParams(vmem_limit_bytes=VMEM_LIMIT)


def shift(n, k):
    return [(i, (i + k) % n) for i in range(n)]


ROUTES = (
    (20, 7, 27, 6, 10, 28, 15, 2, 26, 14, 13, 19, 11, 25, 31, 18, 29, 16, 30, 12, 22, 1, 8, 5, 9, 3, 0, 17, 4, 23, 24, 21),
    (5, 8, 0, 1, 16, 31, 25, 28, 24, 29, 30, 12, 27, 15, 6, 17, 18, 23, 26, 21, 9, 20, 19, 10, 3, 14, 11, 22, 2, 4, 7, 13),
)


def first_hop():
    pairs, sends = [], np.zeros(SIZES, np.int32)
    piece = np.zeros(SIZES, np.int32)
    count = {}
    for zl in range(2):
        for at, pick in enumerate(ROUTES[zl]):
            v, zh, core = np.unravel_index(at, (4, 4, 2))
            u, a, b, zz = np.unravel_index(pick, (4, 2, 2, 2))
            for x in range(4):
                target = ((x + v) % 4, zh, core, x, zl)
                source = (x, 2 * zl + a, b, (x + u) % 4, zz)
                key = (x, zh, zl, 2 * a + b)
                half = count.get(key, 0)
                count[key] = half + 1
                piece[target] = 2 * (2 * a + b) + half
                sends[source] = half
                pairs.append((int(np.ravel_multi_index(source, SIZES)), int(np.ravel_multi_index(target, SIZES))))
    slots = np.zeros(SIZES + (8,), np.int32)
    for at in np.ndindex(*SIZES):
        y, zh, core, x, zl = at
        for i, back in enumerate(BACK):
            for c in range(2):
                slots[at + (piece[(y - back) % 4, zh, (core + c) % 2, x, zl],)] = 2 * i + c
    return sorted(pairs), sends.reshape(-1), slots.reshape(-1, 8)


def spread_kernel(slots, cols, live, tiles, out):
    for b in range(4):
        for s in range(4):
            picks = [jnp.where(live[b, s, k] != 0, cols[b, s, k], -1) for k in range(4)]
            parts = [tiles[b, s, k].astype(F32) for k in range(4)]
            for c in range(4):
                total = jnp.zeros((128, 128), F32)
                for pick, part in zip(picks, parts):
                    total = total + jnp.where(pick == c, part, 0.0)
                slot = slots[2 * s + c // 2]
                out[slot, pl.ds(b * 128, 128), pl.ds((c % 2) * 128, 128)] = total.astype(BF)


def first_terms_kernel(mix, one, two, out):
    out[...] = jnp.dot(mix[0], one[...], preferred_element_type=F32)
    out[...] += jnp.dot(mix[1], two[...], preferred_element_type=F32)


def rest_kernel(mix, begun, *rest):
    parts, out, total = rest[:6], rest[6], rest[7]
    total[...] = begun[...]
    for i, part in enumerate(parts):
        total[...] += jnp.dot(mix[2 + i], part[...], preferred_element_type=F32)
    out[...] = total[...].astype(BF)


def layer_kernel(recv, weight, bias, cot, out, packed):
    total = recv[0].astype(F32)
    for r in range(1, 8):
        total = total + recv[r].astype(F32)
    mixed = total.astype(BF)
    pre = jnp.dot(mixed, weight[...], preferred_element_type=F32) + bias[...]
    sig = jax.nn.sigmoid(pre)
    out[...] = (pre * sig).astype(BF)
    grad = cot[...].astype(F32) * sig * (1.0 + pre * (1.0 - sig))
    low = grad.astype(BF).astype(F32)
    wide = mixed.astype(F32)
    for i in range(4):
        left = wide[:, i * 192 : (i + 1) * 192]
        for j in range(4):
            both = jnp.concatenate([left, low[:, j * 192 : (j + 1) * 192]], axis=1)
            packed[i * 4 + j] = both.astype(BF)


def with_bias(block, row):
    high = row.astype(BF).astype(F32)
    low = row - high
    at = lax.broadcasted_iota(jnp.int32, (8, 384), 0)
    extra = jnp.where(at == 0, high, jnp.where(at == 1, low, 0.0))
    return jnp.concatenate([block, extra], axis=0)


def block_kernel(place, recv, keep, send):
    data = recv[...]
    left = data[:, :192]
    right = data[:, 192:]
    block = lax.dot_general(left, right, (((0,), (0,)), ((), ())), preferred_element_type=F32)
    row = jnp.sum(right.astype(F32), axis=0, keepdims=True)
    row = jnp.concatenate([row, row], axis=1)
    halves = [
        with_bias(
            jnp.concatenate([block[h * 96 : h * 96 + 48], block[h * 96 + 48 : h * 96 + 96]], axis=1),
            row,
        )
        for h in range(2)
    ]
    core = place[1]
    keep[...] = jnp.where(core == 0, halves[0], halves[1])
    send[...] = jnp.where(core == 0, halves[1], halves[0]).astype(BF)


def resplit(total):
    row = total[48:49] + total[49:50]
    return with_bias(total[:48], row).astype(BF)


def pair_kernel(copies, keep, recv, out):
    value = resplit(keep[...] + recv[...].astype(F32))
    for i in range(copies):
        out[i] = value


def sum_kernel(copies, recv, out):
    total = recv[0].astype(F32)
    for r in range(1, 8):
        total = total + recv[r].astype(F32)
    value = resplit(total)
    for i in range(copies):
        out[i] = value


def final_kernel(place, own, other, grad, bias):
    core = place[1]
    for source, at in ((own, core), (other, 1 - core)):
        for i in range(4):
            pieces = [source[i * 4 + j].astype(F32) for j in range(4)]
            for h in range(2):
                rows = jnp.concatenate(
                    [piece[:48, h * 192 : (h + 1) * 192] for piece in pieces], axis=1
                )
                start = pl.multiple_of(i * 192 + at * 96 + h * 48, 16)
                grad[pl.ds(start, 48), :] = rows
    rows = [own[j].astype(F32) for j in range(4)]
    bias[...] = jnp.concatenate([row[48:49, :192] + row[49:50, :192] for row in rows], axis=1)


def call(kernel, shapes, specs, out_specs, scratch=()):
    return pl.pallas_call(
        kernel,
        out_shape=shapes,
        in_specs=specs,
        out_specs=out_specs,
        scratch_shapes=scratch,
        compiler_params=params(),
    )


def struct(shape, dtype):
    return jax.ShapeDtypeStruct(shape, dtype)


def on_device(features, tiles, tile_cols, tile_mask, weight, bias, cotangent):
    place = jnp.stack([lax.axis_index("y"), lax.axis_index("core")]).astype(jnp.int32)
    pairs, sends, slots = first_hop()
    me = lax.axis_index(AXES)
    with jax.named_scope("spread_features"):
        start = lax.dynamic_index_in_dim(jnp.asarray(sends * 256), me, 0, keepdims=False)
        half = lax.dynamic_slice_in_dim(features, start, 256, 0)
        own = lax.ppermute(half, AXES, pairs)
    with jax.named_scope("spread_tiles"):
        mix = call(
            spread_kernel,
            struct((8, 512, 256), BF),
            [smem(), smem(), smem(), vmem()],
            vmem(),
        )(lax.dynamic_index_in_dim(jnp.asarray(slots), me, 0, keepdims=False), tile_cols, tile_mask, tiles)
    own, mix = lax.optimization_barrier((own, mix))
    with jax.named_scope("spread_features"):
        parts = [lax.ppermute(own, "y", shift(4, back)) for back in BACK[1:]]
        own_swapped = lax.ppermute(own, "core", shift(2, 1))
    with jax.named_scope("aggregate"):
        begun = call(first_terms_kernel, struct((512, 768), F32), [vmem()] * 3, vmem())(
            mix, own, own_swapped
        )
    parts[0], begun = lax.optimization_barrier((parts[0], begun))
    with jax.named_scope("spread_features"):
        swapped = [lax.ppermute(part, "core", shift(2, 1)) for part in parts]
        blocks = [block for pair in zip(parts, swapped) for block in pair]
    with jax.named_scope("aggregate"):
        partial = call(
            rest_kernel,
            struct((512, 768), BF),
            [vmem()] * 8,
            vmem(),
            [pltpu.VMEM((512, 768), F32)],
        )(mix, begun, *blocks)
    with jax.named_scope("sum_over_rep"):
        recv = lax.all_to_all(partial, REP, 0, 0, tiled=True).reshape(8, 64, 768)
    with jax.named_scope("layer"):
        output, packed = call(
            layer_kernel,
            (struct((64, 768), BF), struct((16, 64, 384), BF)),
            [vmem()] * 4,
            (vmem(), vmem()),
        )(recv, weight, bias.reshape(1, 768), cotangent)
    with jax.named_scope("exchange_rows"):
        rows = lax.all_to_all(packed.reshape(1024, 384), PLANE, 0, 0, tiled=True)
    with jax.named_scope("weight_block"):
        keep, send = call(
            block_kernel,
            (struct((56, 384), F32), struct((56, 384), BF)),
            [smem(), vmem()],
            (vmem(), vmem()),
        )(place, rows)
        other = lax.ppermute(send, "core", shift(2, 1))
        pair = call(
            lambda *refs: pair_kernel(8, *refs),
            struct((8, 56, 384), BF),
            [vmem()] * 2,
            vmem(),
        )(keep, other)
    with jax.named_scope("sum_over_z"):
        chain = lax.all_to_all(pair.reshape(448, 384), ZAXIS, 0, 0, tiled=True)
        whole = call(
            lambda *refs: sum_kernel(16, *refs),
            struct((16, 56, 384), BF),
            [vmem()],
            vmem(),
        )(chain.reshape(8, 56, 384))
    with jax.named_scope("gather_plane"):
        mine = lax.all_to_all(whole.reshape(896, 384), PLANE, 0, 0, tiled=True)
        theirs = lax.ppermute(mine, "core", shift(2, 1))
    with jax.named_scope("finish"):
        grad_weight, grad_bias = call(
            final_kernel,
            (struct((768, 768), F32), struct((1, 768), F32)),
            [smem(), vmem(), vmem()],
            (vmem(), vmem()),
        )(place, mine.reshape(16, 56, 384), theirs.reshape(16, 56, 384))
    return output, grad_weight, grad_bias.reshape(768)


def solution(mesh):
    fine = Mesh(mesh.devices.reshape(SIZES), AXES)
    placed = (
        P(DOM, None),
        P(DOM, REP, None, None, None),
        P(DOM, REP, None),
        P(DOM, REP, None),
        P(),
        P(),
        P(DOM + REP, None),
    )
    return jax.shard_map(
        on_device,
        mesh=fine,
        in_specs=placed,
        out_specs=(P(DOM + REP, None), P(), P()),
        check_vma=False,
    )
```

```python
import jax
import jax.numpy as jnp
import numpy as np
from jax import lax
from jax.experimental import pallas as pl
from jax.experimental.pallas import tpu as pltpu
from jax.sharding import Mesh, PartitionSpec as P

AXES = ("y", "zh", "core", "x", "zl")
SIZES = (4, 4, 2, 4, 2)
DOM = ("y", "zh", "core")
REP = ("x", "zl")
PLANE = ("x", "y")
ZAXIS = ("zh", "zl")
BF = jnp.bfloat16
F32 = jnp.float32
BACK = (0, 1, 3, 2)
VMEM_LIMIT = 32 * 1024 * 1024

TURN = (((0, 1), (2, 1), (0, 3), (2, 3)), ((2, 3), (2, 3), (0, 1), (0, 1)))
OFFSET = (
    ((2, 1, 0, 3), (2, 3, 1, 0), (0, 3, 2, 1), (3, 1, 0, 2), (1, 0, 3, 2), (1, 2, 3, 0), (0, 2, 1, 3), (3, 0, 2, 1)),
    ((0, 2, 1, 3), (1, 2, 3, 0), (1, 3, 2, 0), (3, 0, 1, 2), (3, 2, 0, 1), (2, 0, 3, 1), (0, 1, 3, 2), (2, 0, 3, 1)),
)


def first_hop():
    pairs = []
    for target in np.ndindex(*SIZES):
        y, zh, core, x, zl = target
        s = (y - x + TURN[zl][zh][core]) % 4
        source = (x, 2 * zl + s // 2, s % 2, (x + OFFSET[zl][2 * s + core][zh]) % 4, core)
        pairs.append((int(np.ravel_multi_index(source, SIZES)), int(np.ravel_multi_index(target, SIZES))))
    return sorted(pairs)


def shift(n, k):
    return [(i, (i + k) % n) for i in range(n)]


def vmem():
    return pl.BlockSpec(memory_space=pltpu.VMEM)


def smem():
    return pl.BlockSpec(memory_space=pltpu.SMEM)


def hbm():
    return pl.BlockSpec(memory_space=pltpu.HBM)


def anyspace():
    return pl.BlockSpec(memory_space=pl.ANY)


def struct(shape, dtype):
    return jax.ShapeDtypeStruct(shape, dtype)


def call(kernel, shapes, specs, out_specs, scratch=(), aliases=None, flops=0):
    return pl.pallas_call(
        kernel,
        out_shape=shapes,
        in_specs=specs,
        out_specs=out_specs,
        scratch_shapes=scratch,
        input_output_aliases=aliases or {},
        compiler_params=pltpu.CompilerParams(vmem_limit_bytes=VMEM_LIMIT),
        cost_estimate=pl.CostEstimate(flops=flops, bytes_accessed=1 << 20, transcendentals=0),
    )


def pick_kernel(features, out, sem):
    start = pl.multiple_of(lax.axis_index("zl") * 384, 384)
    copy = pltpu.make_async_copy(features.at[:, pl.ds(start, 384)], out, sem)
    copy.start()
    copy.wait()


def spread_kernel(picks, other_picks, tiles, other_tiles, out):
    for d, (pick, tile) in enumerate(((picks, tiles), (other_picks, other_tiles))):
        for b in range(4):
            for s in range(4):
                parts = [tile[b, s, k].astype(F32) for k in range(4)]
                for c in range(4):
                    total = jnp.zeros((128, 128), F32)
                    for k in range(4):
                        total = total + jnp.where(pick[b, s, k] == c, parts[k], 0.0)
                    out[d, s, b * 128 : (b + 1) * 128, c * 128 : (c + 1) * 128] = total.astype(BF)


def source_of(back):
    zl, zh, core = lax.axis_index("zl"), lax.axis_index("zh"), lax.axis_index("core")
    turn = jnp.int32(0)
    for i in range(2):
        for j in range(4):
            for k in range(2):
                here = jnp.logical_and(jnp.logical_and(zl == i, zh == j), core == k)
                turn = jnp.where(here, TURN[i][j][k], turn)
    return lax.rem(lax.axis_index("y") - lax.axis_index("x") + turn + 8 - back, 4)


def first_kernel(mix, part, out):
    s = source_of(0)
    for d in range(2):
        out[d] = jnp.dot(mix[d, s], part[...], preferred_element_type=F32)


def next_kernel(back, mix, part, begun, out):
    s = source_of(back)
    for d in range(2):
        out[d] = begun[d] + jnp.dot(mix[d, s], part[...], preferred_element_type=F32)


def last_kernel(back, mix, part, begun, out):
    s = source_of(back)
    core = lax.axis_index("core")
    for d, at in enumerate((core, 1 - core)):
        total = (begun[d] + jnp.dot(mix[d, s], part[...], preferred_element_type=F32)).astype(BF)
        for r in range(8):
            out[r, at] = total[r * 64 : (r + 1) * 64]


def rows_kernel(recv, keep, send):
    total = recv[0].astype(F32)
    for r in range(1, 8):
        total = total + recv[r].astype(F32)
    mixed = total.astype(BF)
    first = lax.axis_index("core") == 0
    keep[...] = jnp.where(first, mixed[0], mixed[1])
    send[...] = jnp.where(first, mixed[1], mixed[0])


def layer_kernel(keep, recv, weight, bias, cot, out, packed):
    first = lax.axis_index("core") == 0
    left = jnp.where(first, keep[...], recv[...])
    right = jnp.where(first, recv[...], keep[...])
    mixed = jnp.concatenate([left, right], axis=1)
    pre = jnp.dot(mixed, weight[...], preferred_element_type=F32) + bias[...]
    sig = jax.nn.sigmoid(pre)
    out[...] = (pre * sig).astype(BF)
    grad = cot[...].astype(F32) * sig * (1.0 + pre * (1.0 - sig))
    low = grad.astype(BF).astype(F32)
    wide = mixed.astype(F32)
    for i in range(4):
        part = wide[:, i * 192 : (i + 1) * 192]
        for j in range(4):
            both = jnp.concatenate([part, low[:, j * 192 : (j + 1) * 192]], axis=1)
            packed[i * 4 + j] = both.astype(BF)


def with_bias(block, row):
    high = row.astype(BF).astype(F32)
    low = row - high
    at = lax.broadcasted_iota(jnp.int32, (8, 384), 0)
    extra = jnp.where(at == 0, high, jnp.where(at == 1, low, 0.0))
    return jnp.concatenate([block, extra], axis=0)


def block_kernel(recv, keep, send):
    data = recv[...]
    left = data[:, :192]
    right = data[:, 192:]
    block = lax.dot_general(left, right, (((0,), (0,)), ((), ())), preferred_element_type=F32)
    row = jnp.sum(right.astype(F32), axis=0, keepdims=True)
    row = jnp.concatenate([row, row], axis=1)
    halves = [
        with_bias(
            jnp.concatenate([block[h * 96 : h * 96 + 48], block[h * 96 + 48 : h * 96 + 96]], axis=1),
            row,
        )
        for h in range(2)
    ]
    first = lax.axis_index("core") == 0
    keep[...] = jnp.where(first, halves[0], halves[1])
    send[...] = jnp.where(first, halves[1], halves[0]).astype(BF)


def resplit(total):
    row = total[48:49] + total[49:50]
    return with_bias(total[:48], row).astype(BF)


def pair_kernel(copies, keep, recv, out):
    value = resplit(keep[...] + recv[...].astype(F32))
    for i in range(copies):
        out[i] = value


def sum_kernel(copies, recv, out):
    total = recv[0].astype(F32)
    for r in range(1, 8):
        total = total + recv[r].astype(F32)
    value = resplit(total)
    for i in range(copies):
        out[i] = value


def write_rows(source, at, grad, rows, sems):
    copies = []
    for i in range(4):
        pieces = [source[i * 4 + j].astype(F32) for j in range(4)]
        for h in range(2):
            rows[i, h * 48 : (h + 1) * 48] = jnp.concatenate(
                [piece[:48, h * 192 : (h + 1) * 192] for piece in pieces], axis=1
            )
        start = pl.multiple_of(i * 192 + at * 96, 32)
        copies.append(pltpu.make_async_copy(rows.at[i], grad.at[pl.ds(start, 96)], sems.at[i]))
        copies[-1].start()
    return copies


def own_half_kernel(own, grad, bias, rows, sems):
    copies = write_rows(own, lax.axis_index("core"), grad, rows, sems)
    parts = [own[j].astype(F32) for j in range(4)]
    bias[...] = jnp.concatenate([part[48:49, :192] + part[49:50, :192] for part in parts], axis=1)
    for copy in copies:
        copy.wait()


def other_half_kernel(other, begun, grad, rows, sems):
    del begun
    for copy in write_rows(other, 1 - lax.axis_index("core"), grad, rows, sems):
        copy.wait()


def on_device(features, tiles, tile_cols, tile_mask, weight, bias, cotangent):
    picks = jnp.where(tile_mask != 0, tile_cols, -1)
    with jax.named_scope("spread_features"):
        half = call(pick_kernel, struct((512, 384), BF), [hbm()], vmem(), [pltpu.SemaphoreType.DMA])(features)
        half, tiles, picks = lax.optimization_barrier((half, tiles, picks))
        own = lax.ppermute(half, AXES, first_hop())
    with jax.named_scope("spread_tiles"):
        other_tiles = lax.ppermute(tiles, "core", shift(2, 1))
        other_picks = lax.ppermute(picks, "core", shift(2, 1))
        mix = call(spread_kernel, struct((2, 4, 512, 512), BF), [smem(), smem(), vmem(), vmem()], vmem())(
            picks, other_picks, tiles, other_tiles
        )
    own, mix = lax.optimization_barrier((own, mix))
    with jax.named_scope("spread_features"):
        parts = [lax.ppermute(own, "y", shift(4, back)) for back in BACK[1:]]
    with jax.named_scope("aggregate"):
        flops = 4 * 512 * 512 * 384
        begun = call(first_kernel, struct((2, 512, 384), F32), [vmem()] * 2, vmem(), flops=flops)(mix, own)
        for back, part in zip(BACK[1:3], parts[:2]):
            begun = call(
                lambda *refs, back=back: next_kernel(back, *refs),
                struct((2, 512, 384), F32),
                [vmem()] * 3,
                vmem(),
                aliases={2: 0},
                flops=flops,
            )(mix, part, begun)
        partial = call(
            lambda *refs: last_kernel(BACK[3], *refs),
            struct((8, 2, 64, 384), BF),
            [vmem()] * 3,
            vmem(),
            flops=flops,
        )(mix, parts[2], begun)
    with jax.named_scope("sum_over_rep"):
        recv = lax.all_to_all(partial, REP, 0, 0, tiled=True)
        keep, send = call(
            rows_kernel, (struct((64, 384), BF), struct((64, 384), BF)), [vmem()], (vmem(), vmem())
        )(recv)
        theirs = lax.ppermute(send, "core", shift(2, 1))
    with jax.named_scope("layer"):
        output, packed = call(
            layer_kernel,
            (struct((64, 768), BF), struct((16, 64, 384), BF)),
            [vmem()] * 5,
            (vmem(), vmem()),
        )(keep, theirs, weight, bias.reshape(1, 768), cotangent)
    with jax.named_scope("exchange_rows"):
        rows = lax.all_to_all(packed.reshape(1024, 384), PLANE, 0, 0, tiled=True)
    with jax.named_scope("weight_block"):
        keep, send = call(
            block_kernel, (struct((56, 384), F32), struct((56, 384), BF)), [vmem()], (vmem(), vmem())
        )(rows)
        other = lax.ppermute(send, "core", shift(2, 1))
        pair = call(lambda *refs: pair_kernel(8, *refs), struct((8, 56, 384), BF), [vmem()] * 2, vmem())(
            keep, other
        )
    with jax.named_scope("sum_over_z"):
        chain = lax.all_to_all(pair.reshape(448, 384), ZAXIS, 0, 0, tiled=True)
        whole = call(lambda *refs: sum_kernel(16, *refs), struct((16, 56, 384), BF), [vmem()], vmem())(
            chain.reshape(8, 56, 384)
        )
    with jax.named_scope("gather_plane"):
        mine = lax.all_to_all(whole.reshape(896, 384), PLANE, 0, 0, tiled=True)
        theirs = lax.ppermute(mine, "core", shift(2, 1))
    with jax.named_scope("finish"):
        scratch = [pltpu.VMEM((4, 96, 768), F32), pltpu.SemaphoreType.DMA((4,))]
        grad, grad_bias = call(
            own_half_kernel,
            (struct((768, 768), F32), struct((1, 768), F32)),
            [vmem()],
            (anyspace(), vmem()),
            scratch,
        )(mine.reshape(16, 56, 384))
        grad_weight = call(
            other_half_kernel,
            struct((768, 768), F32),
            [vmem(), anyspace()],
            anyspace(),
            scratch,
            aliases={1: 0},
        )(theirs.reshape(16, 56, 384), grad)
    return output, grad_weight, grad_bias.reshape(768)


def solution(mesh):
    fine = Mesh(mesh.devices.reshape(SIZES), AXES)
    placed = (
        P(DOM, None),
        P(DOM, REP, None, None, None),
        P(DOM, REP, None),
        P(DOM, REP, None),
        P(),
        P(),
        P(DOM + REP, None),
    )
    return jax.shard_map(
        on_device,
        mesh=fine,
        in_specs=placed,
        out_specs=(P(DOM + REP, None), P(), P()),
        check_vma=False,
    )
```

```python
import jax
import jax.numpy as jnp
import numpy as np
from jax import lax
from jax.experimental import pallas as pl
from jax.experimental.pallas import tpu as pltpu
from jax.sharding import Mesh, PartitionSpec as P

AXES = ("y", "zh", "core", "x", "zl")
SIZES = (4, 4, 2, 4, 2)
DOM = ("y", "zh", "core")
REP = ("x", "zl")
PLANE = ("x", "y")
BF = jnp.bfloat16
F32 = jnp.float32
BACK = (2, 1, 3)
VMEM_LIMIT = 32 * 1024 * 1024

TURN = (((3, 3), (0, 1), (1, 2), (2, 0)), ((2, 0), (3, 3), (1, 2), (0, 1)))
OFFSET = (
    ((1, 2, 3, 0), (2, 1, 0, 3), (2, 0, 1, 3), (3, 2, 0, 1), (2, 3, 1, 0), (0, 1, 2, 3), (0, 2, 3, 1), (1, 0, 2, 3)),
    ((0, 2, 1, 3), (0, 2, 3, 1), (3, 2, 1, 0), (3, 1, 2, 0), (2, 0, 1, 3), (1, 0, 3, 2), (0, 1, 3, 2), (2, 3, 0, 1)),
)


def first_hop():
    pairs = []
    for target in np.ndindex(*SIZES):
        y, zh, core, x, zl = target
        s = (y - x + TURN[zl][zh][core]) % 4
        source = (x, 2 * zl + s // 2, s % 2, (x + OFFSET[zl][2 * s + core][zh]) % 4, core)
        pairs.append((int(np.ravel_multi_index(source, SIZES)), int(np.ravel_multi_index(target, SIZES))))
    return sorted(pairs)


def shift(n, k):
    return [(i, (i + k) % n) for i in range(n)]


def vmem():
    return pl.BlockSpec(memory_space=pltpu.VMEM)


def smem():
    return pl.BlockSpec(memory_space=pltpu.SMEM)


def hbm():
    return pl.BlockSpec(memory_space=pltpu.HBM)


def anyspace():
    return pl.BlockSpec(memory_space=pl.ANY)


def struct(shape, dtype):
    return jax.ShapeDtypeStruct(shape, dtype)


def call(kernel, shapes, specs, out_specs, scratch=(), aliases=None, flops=0):
    return pl.pallas_call(
        kernel,
        out_shape=shapes,
        in_specs=specs,
        out_specs=out_specs,
        scratch_shapes=scratch,
        input_output_aliases=aliases or {},
        compiler_params=pltpu.CompilerParams(vmem_limit_bytes=VMEM_LIMIT),
        cost_estimate=pl.CostEstimate(flops=flops, bytes_accessed=1 << 20, transcendentals=0),
    )


def pick_kernel(features, one, two, sems):
    start = pl.multiple_of(lax.axis_index("zl") * 384, 384)
    copies = [
        pltpu.make_async_copy(features.at[pl.ds(i * 256, 256), pl.ds(start, 384)], out, sems.at[i])
        for i, out in enumerate((one, two))
    ]
    for copy in copies:
        copy.start()
    for copy in copies:
        copy.wait()


def spread_kernel(cols, live, other_cols, other_live, tiles, other_tiles, out):
    for d, (col, on, tile) in enumerate(((cols, live, tiles), (other_cols, other_live, other_tiles))):
        for b in range(4):
            for s in range(4):
                picks = [jnp.where(on[b, s, k] != 0, col[b, s, k], -1) for k in range(4)]
                parts = [tile[b, s, k].astype(F32) for k in range(4)]
                for c in range(4):
                    total = jnp.zeros((128, 128), F32)
                    for pick, part in zip(picks, parts):
                        total = total + jnp.where(pick == c, part, 0.0)
                    out[d, s, b * 128 : (b + 1) * 128, c * 128 : (c + 1) * 128] = total.astype(BF)


def source_of(back):
    zl, zh, core = lax.axis_index("zl"), lax.axis_index("zh"), lax.axis_index("core")
    turn = jnp.int32(0)
    for i in range(2):
        for j in range(4):
            for k in range(2):
                here = jnp.logical_and(jnp.logical_and(zl == i, zh == j), core == k)
                turn = jnp.where(here, TURN[i][j][k], turn)
    return lax.rem(lax.axis_index("y") - lax.axis_index("x") + turn + 8 - back, 4)


def terms(d, mix, keys, parts):
    total = None
    for (back, half), part in zip(keys, parts):
        left = mix[d, source_of(back), :, half * 256 : (half + 1) * 256]
        term = jnp.dot(left, part[...], preferred_element_type=F32)
        total = term if total is None else total + term
    return total


def first_kernel(keys, mix, *refs):
    for d in range(2):
        refs[-1][d] = terms(d, mix, keys, refs[:-1])


def next_kernel(keys, mix, begun, *refs):
    for d in range(2):
        refs[-1][d] = begun[d] + terms(d, mix, keys, refs[:-1])


def last_kernel(keys, mix, begun, *refs):
    core = lax.axis_index("core")
    for d, at in enumerate((core, 1 - core)):
        total = (begun[d] + terms(d, mix, keys, refs[:-1])).astype(BF)
        for r in range(8):
            refs[-1][at, r] = total[r * 64 : (r + 1) * 64]


def layer_kernel(recv, weight, bias, cot, out, packed):
    halves = []
    for c in range(2):
        total = recv[8 * c].astype(F32)
        for r in range(1, 8):
            total = total + recv[8 * c + r].astype(F32)
        halves.append(total.astype(BF))
    mixed = jnp.concatenate(halves, axis=1)
    pre = jnp.dot(mixed, weight[...], preferred_element_type=F32) + bias[...]
    sig = jax.nn.sigmoid(pre)
    out[...] = (pre * sig).astype(BF)
    grad = cot[...].astype(F32) * sig * (1.0 + pre * (1.0 - sig))
    low = grad.astype(BF).astype(F32)
    wide = mixed.astype(F32)
    for i in range(4):
        part = wide[:, i * 192 : (i + 1) * 192]
        for j in range(4):
            both = jnp.concatenate([part, low[:, j * 192 : (j + 1) * 192]], axis=1)
            packed[i * 4 + j] = both.astype(BF)


def with_bias(block, row):
    high = row.astype(BF).astype(F32)
    low = row - high
    at = lax.broadcasted_iota(jnp.int32, (8, 384), 0)
    extra = jnp.where(at == 0, high, jnp.where(at == 1, low, 0.0))
    return jnp.concatenate([block, extra], axis=0)


def block_kernel(recv, keep, send):
    data = recv[...]
    left = data[:, :192]
    right = data[:, 192:]
    block = lax.dot_general(left, right, (((0,), (0,)), ((), ())), preferred_element_type=F32)
    row = jnp.sum(right.astype(F32), axis=0, keepdims=True)
    row = jnp.concatenate([row, row], axis=1)
    halves = [
        with_bias(
            jnp.concatenate([block[h * 96 : h * 96 + 48], block[h * 96 + 48 : h * 96 + 96]], axis=1),
            row,
        )
        for h in range(2)
    ]
    first = lax.axis_index("core") == 0
    keep[...] = jnp.where(first, halves[0], halves[1])
    send[...] = jnp.where(first, halves[1], halves[0]).astype(BF)


def resplit(total):
    row = total[48:49] + total[49:50]
    return with_bias(total[:48], row).astype(BF)


def pair_kernel(keep, recv, out):
    out[...] = resplit(keep[...].astype(F32) + recv[...].astype(F32))


def sum_kernel(copies, own, across, back, ahead, out):
    one = own[...].astype(F32) + across[...].astype(F32)
    two = back[...].astype(F32) + ahead[...].astype(F32)
    value = resplit(one + two)
    for i in range(copies):
        out[i] = value


def write_rows(source, at, grad, rows, sems):
    copies = []
    for i in range(4):
        pieces = [source[i * 4 + j].astype(F32) for j in range(4)]
        for h in range(2):
            rows[i, h * 48 : (h + 1) * 48] = jnp.concatenate(
                [piece[:48, h * 192 : (h + 1) * 192] for piece in pieces], axis=1
            )
        start = pl.multiple_of(i * 192 + at * 96, 32)
        copies.append(pltpu.make_async_copy(rows.at[i], grad.at[pl.ds(start, 96)], sems.at[i]))
        copies[-1].start()
    return copies


def own_half_kernel(own, grad, bias, rows, sems):
    copies = write_rows(own, lax.axis_index("core"), grad, rows, sems)
    parts = [own[j].astype(F32) for j in range(4)]
    bias[...] = jnp.concatenate([part[48:49, :192] + part[49:50, :192] for part in parts], axis=1)
    for copy in copies:
        copy.wait()


def other_half_kernel(other, begun, grad, rows, sems):
    del begun
    for copy in write_rows(other, 1 - lax.axis_index("core"), grad, rows, sems):
        copy.wait()


def product(kernel, keys, mix, parts, begun=None):
    last = kernel is last_kernel
    extra = [] if begun is None else [begun]
    return call(
        lambda *refs: kernel(keys, *refs),
        struct((2, 8, 64, 384), BF) if last else struct((2, 512, 384), F32),
        [vmem()] * (1 + len(extra) + len(parts)),
        vmem(),
        aliases={1: 0} if extra and not last else None,
        flops=4 * 512 * 256 * 384 * len(parts),
    )(mix, *extra, *parts)


def on_device(features, tiles, tile_cols, tile_mask, weight, bias, cotangent):
    with jax.named_scope("spread_features"):
        halves = call(
            pick_kernel,
            (struct((256, 384), BF), struct((256, 384), BF)),
            [hbm()],
            (vmem(), vmem()),
            [pltpu.SemaphoreType.DMA((2,))],
        )(features)
        *halves, tiles = lax.optimization_barrier((*halves, tiles))
        own = [lax.ppermute(half, AXES, first_hop()) for half in halves]
    with jax.named_scope("spread_tiles"):
        there = [lax.ppermute(value, "core", shift(2, 1)) for value in (tiles, tile_cols, tile_mask)]
        own[0], *there = lax.optimization_barrier((own[0], *there))
        mix = call(
            spread_kernel,
            struct((2, 4, 512, 512), BF),
            [smem(), smem(), smem(), smem(), vmem(), vmem()],
            vmem(),
        )(tile_cols, tile_mask, *there[1:], tiles, there[0])
    with jax.named_scope("spread_features"):
        early = [lax.ppermute(own[0], "y", shift(4, back)) for back in BACK]
    own[1], mix = lax.optimization_barrier((own[1], mix))
    with jax.named_scope("spread_features"):
        late = [lax.ppermute(own[1], "y", shift(4, back)) for back in BACK]
    with jax.named_scope("aggregate"):
        begun = product(first_kernel, [(0, 0), (0, 1)], mix, own)
        begun = product(next_kernel, [(back, 0) for back in BACK], mix, early, begun)
        begun = product(next_kernel, [(BACK[0], 1)], mix, late[:1], begun)
        begun = product(next_kernel, [(BACK[1], 1)], mix, late[1:2], begun)
        partial = product(last_kernel, [(BACK[2], 1)], mix, late[2:], begun)
    with jax.named_scope("sum_over_rep"):
        recv = lax.all_to_all(partial.reshape(1024, 384), ("core",) + REP, 0, 0, tiled=True)
    with jax.named_scope("layer"):
        output, packed = call(
            layer_kernel,
            (struct((64, 768), BF), struct((16, 64, 384), BF)),
            [vmem()] * 4,
            (vmem(), vmem()),
        )(recv.reshape(16, 64, 384), weight, bias.reshape(1, 768), cotangent)
    with jax.named_scope("exchange_rows"):
        rows = lax.all_to_all(packed.reshape(1024, 384), PLANE, 0, 0, tiled=True)
    with jax.named_scope("weight_block"):
        keep, send = call(
            block_kernel, (struct((56, 384), F32), struct((56, 384), BF)), [vmem()], (vmem(), vmem())
        )(rows)
        other = lax.ppermute(send, "core", shift(2, 1))
        pair = call(pair_kernel, struct((56, 384), BF), [vmem()] * 2, vmem())(keep, other)
    with jax.named_scope("sum_over_z"):
        beside = lax.ppermute(pair, "zl", shift(2, 1))
        pair = call(pair_kernel, struct((56, 384), BF), [vmem()] * 2, vmem())(pair, beside)
        chain = [lax.ppermute(pair, "zh", shift(4, back)) for back in BACK]
        whole = call(lambda *refs: sum_kernel(16, *refs), struct((16, 56, 384), BF), [vmem()] * 4, vmem())(
            pair, *chain
        )
    with jax.named_scope("gather_plane"):
        mine = lax.all_to_all(whole.reshape(896, 384), PLANE, 0, 0, tiled=True)
        theirs = lax.ppermute(mine, "core", shift(2, 1))
    with jax.named_scope("finish"):
        scratch = [pltpu.VMEM((4, 96, 768), F32), pltpu.SemaphoreType.DMA((4,))]
        grad, grad_bias = call(
            own_half_kernel,
            (struct((768, 768), F32), struct((1, 768), F32)),
            [vmem()],
            (anyspace(), vmem()),
            scratch,
        )(mine.reshape(16, 56, 384))
        grad_weight = call(
            other_half_kernel,
            struct((768, 768), F32),
            [vmem(), anyspace()],
            anyspace(),
            scratch,
            aliases={1: 0},
        )(theirs.reshape(16, 56, 384), grad)
    return output, grad_weight, grad_bias.reshape(768)


def solution(mesh):
    fine = Mesh(mesh.devices.reshape(SIZES), AXES)
    placed = (
        P(DOM, None),
        P(DOM, REP, None, None, None),
        P(DOM, REP, None),
        P(DOM, REP, None),
        P(),
        P(),
        P(DOM + REP, None),
    )
    return jax.shard_map(
        on_device,
        mesh=fine,
        in_specs=placed,
        out_specs=(P(DOM + REP, None), P(), P()),
        check_vma=False,
    )
```

```python
import jax
import jax.numpy as jnp
import numpy as np
from jax import lax
from jax.experimental import pallas as pl
from jax.experimental.pallas import tpu as pltpu
from jax.sharding import Mesh, PartitionSpec as P

AXES = ("y", "zh", "core", "x", "zl")
SIZES = (4, 4, 2, 4, 2)
DOM = ("y", "zh", "core")
REP = ("x", "zl")
PLANE = ("x", "y")
BF = jnp.bfloat16
F32 = jnp.float32
BACK = (2, 1, 3)
VMEM_LIMIT = 32 * 1024 * 1024

TURN = (((3, 3), (0, 1), (1, 2), (2, 0)), ((2, 0), (3, 3), (1, 2), (0, 1)))
OFFSET = (
    ((1, 2, 3, 0), (2, 1, 0, 3), (2, 0, 1, 3), (3, 2, 0, 1), (2, 3, 1, 0), (0, 1, 2, 3), (0, 2, 3, 1), (1, 0, 2, 3)),
    ((0, 2, 1, 3), (0, 2, 3, 1), (3, 2, 1, 0), (3, 1, 2, 0), (2, 0, 1, 3), (1, 0, 3, 2), (0, 1, 3, 2), (2, 3, 0, 1)),
)


def first_hop():
    pairs = []
    for target in np.ndindex(*SIZES):
        y, zh, core, x, zl = target
        s = (y - x + TURN[zl][zh][core]) % 4
        source = (x, 2 * zl + s // 2, s % 2, (x + OFFSET[zl][2 * s + core][zh]) % 4, core)
        pairs.append((int(np.ravel_multi_index(source, SIZES)), int(np.ravel_multi_index(target, SIZES))))
    return sorted(pairs)


def shift(n, k):
    return [(i, (i + k) % n) for i in range(n)]


def vmem():
    return pl.BlockSpec(memory_space=pltpu.VMEM)


def smem():
    return pl.BlockSpec(memory_space=pltpu.SMEM)


def hbm():
    return pl.BlockSpec(memory_space=pltpu.HBM)


def anyspace():
    return pl.BlockSpec(memory_space=pl.ANY)


def struct(shape, dtype):
    return jax.ShapeDtypeStruct(shape, dtype)


def call(kernel, shapes, specs, out_specs, scratch=(), aliases=None, flops=0):
    return pl.pallas_call(
        kernel,
        out_shape=shapes,
        in_specs=specs,
        out_specs=out_specs,
        scratch_shapes=scratch,
        input_output_aliases=aliases or {},
        compiler_params=pltpu.CompilerParams(vmem_limit_bytes=VMEM_LIMIT),
        cost_estimate=pl.CostEstimate(flops=flops, bytes_accessed=1 << 20, transcendentals=0),
    )


def pick_kernel(features, one, two, sems):
    start = pl.multiple_of(lax.axis_index("zl") * 384, 384)
    copies = [
        pltpu.make_async_copy(features.at[pl.ds(i * 256, 256), pl.ds(start, 384)], out, sems.at[i])
        for i, out in enumerate((one, two))
    ]
    for copy in copies:
        copy.start()
    for copy in copies:
        copy.wait()


def spread_kernel(cols, live, other_cols, other_live, tiles, other_tiles, out):
    for d, (col, on, tile) in enumerate(((cols, live, tiles), (other_cols, other_live, other_tiles))):
        for b in range(4):
            for s in range(4):
                picks = [jnp.where(on[b, s, k] != 0, col[b, s, k], -1) for k in range(4)]
                parts = [tile[b, s, k].astype(F32) for k in range(4)]
                for c in range(4):
                    total = jnp.zeros((128, 128), F32)
                    for pick, part in zip(picks, parts):
                        total = total + jnp.where(pick == c, part, 0.0)
                    out[d, s, b * 128 : (b + 1) * 128, c * 128 : (c + 1) * 128] = total.astype(BF)


def source_of(back):
    zl, zh, core = lax.axis_index("zl"), lax.axis_index("zh"), lax.axis_index("core")
    turn = jnp.int32(0)
    for i in range(2):
        for j in range(4):
            for k in range(2):
                here = jnp.logical_and(jnp.logical_and(zl == i, zh == j), core == k)
                turn = jnp.where(here, TURN[i][j][k], turn)
    return lax.rem(lax.axis_index("y") - lax.axis_index("x") + turn + 8 - back, 4)


def terms(d, mix, keys, parts):
    total = None
    for (back, half), part in zip(keys, parts):
        left = mix[d, source_of(back), :, half * 256 : (half + 1) * 256]
        term = jnp.dot(left, part[...], preferred_element_type=F32)
        total = term if total is None else total + term
    return total


def first_kernel(keys, mix, *refs):
    for d in range(2):
        refs[-1][d] = terms(d, mix, keys, refs[:-1])


def next_kernel(keys, mix, begun, *refs):
    for d in range(2):
        refs[-1][d] = begun[d] + terms(d, mix, keys, refs[:-1])


def last_kernel(keys, mix, begun, *refs):
    core = lax.axis_index("core")
    for d, at in enumerate((core, 1 - core)):
        total = (begun[d] + terms(d, mix, keys, refs[:-1])).astype(BF)
        for r in range(8):
            refs[-1][at, r] = total[r * 64 : (r + 1) * 64]


def layer_kernel(recv, weight, bias, cot, out, packed):
    halves = []
    for c in range(2):
        total = recv[8 * c].astype(F32)
        for r in range(1, 8):
            total = total + recv[8 * c + r].astype(F32)
        halves.append(total.astype(BF))
    mixed = jnp.concatenate(halves, axis=1)
    pre = jnp.dot(mixed, weight[...], preferred_element_type=F32) + bias[...]
    sig = jax.nn.sigmoid(pre)
    out[...] = (pre * sig).astype(BF)
    grad = cot[...].astype(F32) * sig * (1.0 + pre * (1.0 - sig))
    low = grad.astype(BF).astype(F32)
    wide = mixed.astype(F32)
    for i in range(4):
        part = wide[:, i * 192 : (i + 1) * 192]
        for j in range(4):
            both = jnp.concatenate([part, low[:, j * 192 : (j + 1) * 192]], axis=1)
            packed[i * 4 + j] = both.astype(BF)


def with_bias(block, row):
    high = row.astype(BF).astype(F32)
    low = row - high
    at = lax.broadcasted_iota(jnp.int32, (8, 384), 0)
    extra = jnp.where(at == 0, high, jnp.where(at == 1, low, 0.0))
    return jnp.concatenate([block, extra], axis=0)


def block_kernel(recv, keep, send):
    data = recv[...]
    left = data[:, :192]
    right = data[:, 192:]
    block = lax.dot_general(left, right, (((0,), (0,)), ((), ())), preferred_element_type=F32)
    row = jnp.sum(right.astype(F32), axis=0, keepdims=True)
    row = jnp.concatenate([row, row], axis=1)
    halves = [
        with_bias(
            jnp.concatenate([block[h * 96 : h * 96 + 48], block[h * 96 + 48 : h * 96 + 96]], axis=1),
            row,
        ).astype(BF)
        for h in range(2)
    ]
    first = lax.axis_index("core") == 0
    keep[...] = jnp.where(first, halves[0], halves[1])
    send[...] = jnp.where(first, halves[1], halves[0])


def resplit(total):
    row = total[48:49] + total[49:50]
    return with_bias(total[:48], row).astype(BF)


def four_kernel(copies, one, two, three, four, out):
    total = (one[...].astype(F32) + two[...].astype(F32)) + (three[...].astype(F32) + four[...].astype(F32))
    value = resplit(total)
    if copies is None:
        out[...] = value
    else:
        for i in range(copies):
            out[i] = value


def write_rows(source, at, grad, rows, sems):
    copies = []
    for i in range(4):
        pieces = [source[i * 4 + j].astype(F32) for j in range(4)]
        for h in range(2):
            rows[i, h * 48 : (h + 1) * 48] = jnp.concatenate(
                [piece[:48, h * 192 : (h + 1) * 192] for piece in pieces], axis=1
            )
        start = pl.multiple_of(i * 192 + at * 96, 32)
        copies.append(pltpu.make_async_copy(rows.at[i], grad.at[pl.ds(start, 96)], sems.at[i]))
        copies[-1].start()
    return copies


def own_half_kernel(own, grad, bias, rows, sems):
    copies = write_rows(own, lax.axis_index("core"), grad, rows, sems)
    parts = [own[j].astype(F32) for j in range(4)]
    bias[...] = jnp.concatenate([part[48:49, :192] + part[49:50, :192] for part in parts], axis=1)
    for copy in copies:
        copy.wait()


def other_half_kernel(other, begun, grad, rows, sems):
    del begun
    for copy in write_rows(other, 1 - lax.axis_index("core"), grad, rows, sems):
        copy.wait()


def product(kernel, keys, mix, parts, begun=None):
    last = kernel is last_kernel
    extra = [] if begun is None else [begun]
    return call(
        lambda *refs: kernel(keys, *refs),
        struct((2, 8, 64, 384), BF) if last else struct((2, 512, 384), F32),
        [vmem()] * (1 + len(extra) + len(parts)),
        vmem(),
        aliases={1: 0} if extra and not last else None,
        flops=4 * 512 * 256 * 384 * len(parts),
    )(mix, *extra, *parts)


def on_device(features, tiles, tile_cols, tile_mask, weight, bias, cotangent):
    with jax.named_scope("spread_features"):
        halves = call(
            pick_kernel,
            (struct((256, 384), BF), struct((256, 384), BF)),
            [hbm()],
            (vmem(), vmem()),
            [pltpu.SemaphoreType.DMA((2,))],
        )(features)
        *halves, tiles = lax.optimization_barrier((*halves, tiles))
        own = [lax.ppermute(half, AXES, first_hop()) for half in halves]
    with jax.named_scope("spread_tiles"):
        there = [lax.ppermute(value, "core", shift(2, 1)) for value in (tiles, tile_cols, tile_mask)]
        mix = call(
            spread_kernel,
            struct((2, 4, 512, 512), BF),
            [smem(), smem(), smem(), smem(), vmem(), vmem()],
            vmem(),
        )(tile_cols, tile_mask, *there[1:], tiles, there[0])
    own[0], mix = lax.optimization_barrier((own[0], mix))
    with jax.named_scope("spread_features"):
        early = [lax.ppermute(own[0], "y", shift(4, back)) for back in BACK]
    with jax.named_scope("spread_features"):
        late = [lax.ppermute(own[1], "y", shift(4, back)) for back in BACK]
    with jax.named_scope("aggregate"):
        begun = product(first_kernel, [(0, 0), (0, 1)], mix, own)
        begun = product(next_kernel, [(back, 0) for back in BACK], mix, early, begun)
        begun = product(next_kernel, [(BACK[0], 1)], mix, late[:1], begun)
        begun = product(next_kernel, [(BACK[1], 1)], mix, late[1:2], begun)
        partial = product(last_kernel, [(BACK[2], 1)], mix, late[2:], begun)
    with jax.named_scope("sum_over_rep"):
        recv = lax.all_to_all(partial.reshape(1024, 384), ("core",) + REP, 0, 0, tiled=True)
    with jax.named_scope("layer"):
        output, packed = call(
            layer_kernel,
            (struct((64, 768), BF), struct((16, 64, 384), BF)),
            [vmem()] * 4,
            (vmem(), vmem()),
        )(recv.reshape(16, 64, 384), weight, bias.reshape(1, 768), cotangent)
    with jax.named_scope("exchange_rows"):
        rows = lax.all_to_all(packed.reshape(1024, 384), PLANE, 0, 0, tiled=True)
    with jax.named_scope("weight_block"):
        keep, send = call(
            block_kernel, (struct((56, 384), BF), struct((56, 384), BF)), [vmem()], (vmem(), vmem())
        )(rows)
        beside = lax.ppermute(keep, "zl", shift(2, 1))
        across = lax.ppermute(send, ("core", "zl"), [(0, 3), (1, 2), (2, 1), (3, 0)])
        other = lax.ppermute(send, "core", shift(2, 1))
        pair = call(
            lambda *refs: four_kernel(None, *refs), struct((56, 384), BF), [vmem()] * 4, vmem()
        )(keep, other, beside, across)
    with jax.named_scope("sum_over_z"):
        chain = [lax.ppermute(pair, "zh", shift(4, back)) for back in BACK]
        whole = call(
            lambda *refs: four_kernel(16, *refs), struct((16, 56, 384), BF), [vmem()] * 4, vmem()
        )(pair, *chain)
    with jax.named_scope("gather_plane"):
        mine = lax.all_to_all(whole.reshape(896, 384), PLANE, 0, 0, tiled=True)
        theirs = lax.ppermute(mine, "core", shift(2, 1))
    with jax.named_scope("finish"):
        scratch = [pltpu.VMEM((4, 96, 768), F32), pltpu.SemaphoreType.DMA((4,))]
        grad, grad_bias = call(
            own_half_kernel,
            (struct((768, 768), F32), struct((1, 768), F32)),
            [vmem()],
            (anyspace(), vmem()),
            scratch,
        )(mine.reshape(16, 56, 384))
        grad_weight = call(
            other_half_kernel,
            struct((768, 768), F32),
            [vmem(), anyspace()],
            anyspace(),
            scratch,
            aliases={1: 0},
        )(theirs.reshape(16, 56, 384), grad)
    return output, grad_weight, grad_bias.reshape(768)


def solution(mesh):
    fine = Mesh(mesh.devices.reshape(SIZES), AXES)
    placed = (
        P(DOM, None),
        P(DOM, REP, None, None, None),
        P(DOM, REP, None),
        P(DOM, REP, None),
        P(),
        P(),
        P(DOM + REP, None),
    )
    return jax.shard_map(
        on_device,
        mesh=fine,
        in_specs=placed,
        out_specs=(P(DOM + REP, None), P(), P()),
        check_vma=False,
    )
```

```python
import jax
import jax.numpy as jnp
import numpy as np
from jax import lax
from jax.experimental import pallas as pl
from jax.experimental.pallas import tpu as pltpu
from jax.sharding import Mesh, PartitionSpec as P

AXES = ("y", "zh", "core", "x", "zl")
SIZES = (4, 4, 2, 4, 2)
DOM = ("y", "zh", "core")
REP = ("x", "zl")
PLANE = ("x", "y")
BF = jnp.bfloat16
F32 = jnp.float32
BACK = (2, 1, 3)
VMEM_LIMIT = 32 * 1024 * 1024

TURN = (((3, 3), (0, 1), (1, 2), (2, 0)), ((2, 0), (3, 3), (1, 2), (0, 1)))
OFFSET = (
    ((1, 2, 3, 0), (2, 1, 0, 3), (2, 0, 1, 3), (3, 2, 0, 1), (2, 3, 1, 0), (0, 1, 2, 3), (0, 2, 3, 1), (1, 0, 2, 3)),
    ((0, 2, 1, 3), (0, 2, 3, 1), (3, 2, 1, 0), (3, 1, 2, 0), (2, 0, 1, 3), (1, 0, 3, 2), (0, 1, 3, 2), (2, 3, 0, 1)),
)


def first_hop():
    pairs = []
    for target in np.ndindex(*SIZES):
        y, zh, core, x, zl = target
        s = (y - x + TURN[zl][zh][core]) % 4
        source = (x, 2 * zl + s // 2, s % 2, (x + OFFSET[zl][2 * s + core][zh]) % 4, core)
        pairs.append((int(np.ravel_multi_index(source, SIZES)), int(np.ravel_multi_index(target, SIZES))))
    return sorted(pairs)


def shift(n, k):
    return [(i, (i + k) % n) for i in range(n)]


def vmem():
    return pl.BlockSpec(memory_space=pltpu.VMEM)


def smem():
    return pl.BlockSpec(memory_space=pltpu.SMEM)


def hbm():
    return pl.BlockSpec(memory_space=pltpu.HBM)


def anyspace():
    return pl.BlockSpec(memory_space=pl.ANY)


def struct(shape, dtype):
    return jax.ShapeDtypeStruct(shape, dtype)


def call(kernel, shapes, specs, out_specs, scratch=(), aliases=None, flops=0, limit=VMEM_LIMIT):
    return pl.pallas_call(
        kernel,
        out_shape=shapes,
        in_specs=specs,
        out_specs=out_specs,
        scratch_shapes=scratch,
        input_output_aliases=aliases or {},
        compiler_params=pltpu.CompilerParams(vmem_limit_bytes=limit),
        cost_estimate=pl.CostEstimate(flops=flops, bytes_accessed=1 << 20, transcendentals=0),
    )


def pick_kernel(features, one, two, sems):
    start = pl.multiple_of(lax.axis_index("zl") * 384, 384)
    copies = [
        pltpu.make_async_copy(features.at[pl.ds(i * 256, 256), pl.ds(start, 384)], out, sems.at[i])
        for i, out in enumerate((one, two))
    ]
    for copy in copies:
        copy.start()
    for copy in copies:
        copy.wait()


def spread_kernel(cols, live, other_cols, other_live, tiles, other_tiles, out):
    for d, (col, on, tile) in enumerate(((cols, live, tiles), (other_cols, other_live, other_tiles))):
        for b in range(4):
            for s in range(4):
                picks = [jnp.where(on[b, s, k] != 0, col[b, s, k], -1) for k in range(4)]
                parts = [tile[b, s, k].astype(F32) for k in range(4)]
                for c in range(4):
                    total = jnp.zeros((128, 128), F32)
                    for pick, part in zip(picks, parts):
                        total = total + jnp.where(pick == c, part, 0.0)
                    out[d, s, b * 128 : (b + 1) * 128, c * 128 : (c + 1) * 128] = total.astype(BF)


def source_of(back):
    zl, zh, core = lax.axis_index("zl"), lax.axis_index("zh"), lax.axis_index("core")
    turn = jnp.int32(0)
    for i in range(2):
        for j in range(4):
            for k in range(2):
                here = jnp.logical_and(jnp.logical_and(zl == i, zh == j), core == k)
                turn = jnp.where(here, TURN[i][j][k], turn)
    return lax.rem(lax.axis_index("y") - lax.axis_index("x") + turn + 8 - back, 4)


def terms(d, mix, keys, parts):
    total = None
    for (back, half), part in zip(keys, parts):
        left = mix[d, source_of(back), :, half * 256 : (half + 1) * 256]
        term = jnp.dot(left, part[...], preferred_element_type=F32)
        total = term if total is None else total + term
    return total


def first_kernel(keys, mix, *refs):
    for d in range(2):
        refs[-1][d] = terms(d, mix, keys, refs[:-1])


def next_kernel(keys, mix, begun, *refs):
    for d in range(2):
        refs[-1][d] = begun[d] + terms(d, mix, keys, refs[:-1])


def last_kernel(keys, mix, begun, *refs):
    core = lax.axis_index("core")
    for d, at in enumerate((core, 1 - core)):
        refs[-1][at] = (begun[d] + terms(d, mix, keys, refs[:-1])).astype(BF)


def layer_kernel(recv, weight, bias, cot, out, packed):
    halves = []
    for c in range(2):
        total = recv[8 * c].astype(F32)
        for r in range(1, 8):
            total = total + recv[8 * c + r].astype(F32)
        halves.append(total.astype(BF))
    mixed = jnp.concatenate(halves, axis=1)
    pre = jnp.dot(mixed, weight[...], preferred_element_type=F32) + bias[...]
    sig = jax.nn.sigmoid(pre)
    out[...] = (pre * sig).astype(BF)
    grad = cot[...].astype(F32) * sig * (1.0 + pre * (1.0 - sig))
    low = grad.astype(BF).astype(F32)
    wide = mixed.astype(F32)
    for i in range(4):
        part = wide[:, i * 192 : (i + 1) * 192]
        for j in range(4):
            both = jnp.concatenate([part, low[:, j * 192 : (j + 1) * 192]], axis=1)
            packed[i * 4 + j] = both.astype(BF)


def with_bias(block, row):
    high = row.astype(BF).astype(F32)
    low = row - high
    at = lax.broadcasted_iota(jnp.int32, (8, 384), 0)
    extra = jnp.where(at == 0, high, jnp.where(at == 1, low, 0.0))
    return jnp.concatenate([block, extra], axis=0)


def block_kernel(recv, keep, send):
    data = recv[...]
    left = data[:, :192]
    right = data[:, 192:]
    block = lax.dot_general(left, right, (((0,), (0,)), ((), ())), preferred_element_type=F32)
    row = jnp.sum(right.astype(F32), axis=0, keepdims=True)
    row = jnp.concatenate([row, row], axis=1)
    halves = [
        with_bias(
            jnp.concatenate([block[h * 96 : h * 96 + 48], block[h * 96 + 48 : h * 96 + 96]], axis=1),
            row,
        ).astype(BF)
        for h in range(2)
    ]
    first = lax.axis_index("core") == 0
    keep[...] = jnp.where(first, halves[0], halves[1])
    send[...] = jnp.where(first, halves[1], halves[0])


def resplit(total):
    row = total[48:49] + total[49:50]
    return with_bias(total[:48], row).astype(BF)


def four_kernel(copies, one, two, three, four, out):
    total = (one[...].astype(F32) + two[...].astype(F32)) + (three[...].astype(F32) + four[...].astype(F32))
    value = resplit(total)
    if copies is None:
        out[...] = value
    else:
        for i in range(copies):
            out[i] = value


def write_rows(source, at, grad, rows, sems):
    copies = []
    for i in range(4):
        pieces = [source[i * 4 + j].astype(F32) for j in range(4)]
        for h in range(2):
            rows[i, h * 48 : (h + 1) * 48] = jnp.concatenate(
                [piece[:48, h * 192 : (h + 1) * 192] for piece in pieces], axis=1
            )
        start = pl.multiple_of(i * 192 + at * 96, 32)
        copies.append(pltpu.make_async_copy(rows.at[i], grad.at[pl.ds(start, 96)], sems.at[i]))
        copies[-1].start()
    return copies


def own_half_kernel(own, grad, bias, rows, sems):
    copies = write_rows(own, lax.axis_index("core"), grad, rows, sems)
    parts = [own[j].astype(F32) for j in range(4)]
    bias[...] = jnp.concatenate([part[48:49, :192] + part[49:50, :192] for part in parts], axis=1)
    for copy in copies:
        copy.wait()


def other_half_kernel(other, begun, grad, rows, sems):
    del begun
    for copy in write_rows(other, 1 - lax.axis_index("core"), grad, rows, sems):
        copy.wait()


def product(kernel, keys, mix, parts, begun=None):
    last = kernel is last_kernel
    extra = [] if begun is None else [begun]
    return call(
        lambda *refs: kernel(keys, *refs),
        struct((2, 512, 384), BF) if last else struct((2, 512, 384), F32),
        [vmem()] * (1 + len(extra) + len(parts)),
        vmem(),
        aliases={1: 0} if extra and not last else None,
        flops=4 * 512 * 256 * 384 * len(parts),
    )(mix, *extra, *parts)


def on_device(features, tiles, tile_cols, tile_mask, weight, bias, cotangent):
    with jax.named_scope("spread_features"):
        halves = call(
            pick_kernel,
            (struct((256, 384), BF), struct((256, 384), BF)),
            [hbm()],
            (vmem(), vmem()),
            [pltpu.SemaphoreType.DMA((2,))],
            limit=60 * 1024 * 1024,
        )(features)
        *halves, tiles = lax.optimization_barrier((*halves, tiles))
        own = [lax.ppermute(half, AXES, first_hop()) for half in halves]
    with jax.named_scope("spread_tiles"):
        there = [lax.ppermute(value, "core", shift(2, 1)) for value in (tiles, tile_cols, tile_mask)]
        mix = call(
            spread_kernel,
            struct((2, 4, 512, 512), BF),
            [smem(), smem(), smem(), smem(), vmem(), vmem()],
            vmem(),
        )(tile_cols, tile_mask, *there[1:], tiles, there[0])
    own[0], mix = lax.optimization_barrier((own[0], mix))
    with jax.named_scope("spread_features"):
        early = [lax.ppermute(own[0], "y", shift(4, back)) for back in BACK]
    with jax.named_scope("spread_features"):
        late = [lax.ppermute(own[1], "y", shift(4, back)) for back in BACK]
    with jax.named_scope("aggregate"):
        begun = product(first_kernel, [(0, 0), (0, 1)], mix, own)
        begun = product(next_kernel, [(back, 0) for back in BACK], mix, early, begun)
        begun = product(next_kernel, [(BACK[0], 1)], mix, late[:1], begun)
        begun = product(next_kernel, [(BACK[1], 1)], mix, late[1:2], begun)
        partial = product(last_kernel, [(BACK[2], 1)], mix, late[2:], begun)
    with jax.named_scope("sum_over_rep"):
        recv = lax.all_to_all(partial.reshape(1024, 384), ("core",) + REP, 0, 0, tiled=True)
    with jax.named_scope("layer"):
        output, packed = call(
            layer_kernel,
            (struct((64, 768), BF), struct((16, 64, 384), BF)),
            [vmem()] * 4,
            (vmem(), vmem()),
        )(recv.reshape(16, 64, 384), weight, bias.reshape(1, 768), cotangent)
    with jax.named_scope("exchange_rows"):
        rows = lax.all_to_all(packed.reshape(1024, 384), PLANE, 0, 0, tiled=True)
    with jax.named_scope("weight_block"):
        keep, send = call(
            block_kernel, (struct((56, 384), BF), struct((56, 384), BF)), [vmem()], (vmem(), vmem())
        )(rows)
        beside = lax.ppermute(keep, "zl", shift(2, 1))
        across = lax.ppermute(send, ("core", "zl"), [(0, 3), (1, 2), (2, 1), (3, 0)])
        other = lax.ppermute(send, "core", shift(2, 1))
        pair = call(
            lambda *refs: four_kernel(None, *refs), struct((56, 384), BF), [vmem()] * 4, vmem()
        )(keep, other, beside, across)
    with jax.named_scope("sum_over_z"):
        chain = [lax.ppermute(pair, "zh", shift(4, back)) for back in BACK]
        whole = call(
            lambda *refs: four_kernel(16, *refs), struct((16, 56, 384), BF), [vmem()] * 4, vmem()
        )(pair, *chain)
    with jax.named_scope("gather_plane"):
        mine = lax.all_to_all(whole.reshape(896, 384), PLANE, 0, 0, tiled=True)
        theirs = lax.ppermute(mine, "core", shift(2, 1))
    with jax.named_scope("finish"):
        scratch = [pltpu.VMEM((4, 96, 768), F32), pltpu.SemaphoreType.DMA((4,))]
        grad, grad_bias = call(
            own_half_kernel,
            (struct((768, 768), F32), struct((1, 768), F32)),
            [vmem()],
            (anyspace(), vmem()),
            scratch,
        )(mine.reshape(16, 56, 384))
        grad_weight = call(
            other_half_kernel,
            struct((768, 768), F32),
            [vmem(), anyspace()],
            anyspace(),
            scratch,
            aliases={1: 0},
        )(theirs.reshape(16, 56, 384), grad)
    return output, grad_weight, grad_bias.reshape(768)


def solution(mesh):
    fine = Mesh(mesh.devices.reshape(SIZES), AXES)
    placed = (
        P(DOM, None),
        P(DOM, REP, None, None, None),
        P(DOM, REP, None),
        P(DOM, REP, None),
        P(),
        P(),
        P(DOM + REP, None),
    )
    return jax.shard_map(
        on_device,
        mesh=fine,
        in_specs=placed,
        out_specs=(P(DOM + REP, None), P(), P()),
        check_vma=False,
    )
```

```python
import jax
import jax.numpy as jnp
import numpy as np
from jax import lax
from jax.experimental import pallas as pl
from jax.experimental.pallas import tpu as pltpu
from jax.sharding import Mesh, PartitionSpec as P

AXES = ("y", "zh", "core", "x", "zl")
SIZES = (4, 4, 2, 4, 2)
DOM = ("y", "zh", "core")
REP = ("x", "zl")
PLANE = ("x", "y")
BF = jnp.bfloat16
F32 = jnp.float32
BACK = (2, 1, 3)
VMEM_LIMIT = 32 * 1024 * 1024

TURN = (((1, 3), (3, 1), (1, 3), (3, 1)), ((2, 0), (0, 2), (2, 0), (0, 2)))
OFFSET = (
    ((2, 3, 0, 1), (2, 1, 0, 3), (2, 1, 3, 0), (1, 3, 0, 2), (1, 0, 2, 3), (0, 2, 3, 1), (0, 2, 1, 3), (3, 1, 2, 0)),
    ((0, 2, 3, 1), (3, 1, 2, 0), (3, 2, 1, 0), (0, 3, 1, 2), (2, 0, 1, 3), (2, 3, 0, 1), (1, 0, 2, 3), (1, 0, 3, 2)),
)


def first_hop():
    pairs = []
    for target in np.ndindex(*SIZES):
        y, zh, core, x, zl = target
        s = (y - x + TURN[zl][zh][core]) % 4
        source = (x, 2 * zl + s // 2, s % 2, (x + OFFSET[zl][2 * s + core][zh]) % 4, core)
        pairs.append((int(np.ravel_multi_index(source, SIZES)), int(np.ravel_multi_index(target, SIZES))))
    return sorted(pairs)


def shift(n, k):
    return [(i, (i + k) % n) for i in range(n)]


def vmem():
    return pl.BlockSpec(memory_space=pltpu.VMEM)


def smem():
    return pl.BlockSpec(memory_space=pltpu.SMEM)


def hbm():
    return pl.BlockSpec(memory_space=pltpu.HBM)


def anyspace():
    return pl.BlockSpec(memory_space=pl.ANY)


def struct(shape, dtype):
    return jax.ShapeDtypeStruct(shape, dtype)


def call(kernel, shapes, specs, out_specs, scratch=(), aliases=None, flops=0):
    return pl.pallas_call(
        kernel,
        out_shape=shapes,
        in_specs=specs,
        out_specs=out_specs,
        scratch_shapes=scratch,
        input_output_aliases=aliases or {},
        compiler_params=pltpu.CompilerParams(vmem_limit_bytes=VMEM_LIMIT),
        cost_estimate=pl.CostEstimate(flops=flops, bytes_accessed=1 << 20, transcendentals=0),
    )


def pick_kernel(features, one, two, sems):
    start = pl.multiple_of(lax.axis_index("zl") * 384, 384)
    copies = [
        pltpu.make_async_copy(features.at[pl.ds(i * 256, 256), pl.ds(start, 384)], out, sems.at[i])
        for i, out in enumerate((one, two))
    ]
    for copy in copies:
        copy.start()
    for copy in copies:
        copy.wait()


def spread_kernel(cols, live, other_cols, other_live, tiles, other_tiles, out):
    for d, (col, on, tile) in enumerate(((cols, live, tiles), (other_cols, other_live, other_tiles))):
        for b in range(4):
            for s in range(4):
                picks = [jnp.where(on[b, s, k] != 0, col[b, s, k], -1) for k in range(4)]
                parts = [tile[b, s, k].astype(F32) for k in range(4)]
                for c in range(4):
                    total = jnp.zeros((128, 128), F32)
                    for pick, part in zip(picks, parts):
                        total = total + jnp.where(pick == c, part, 0.0)
                    out[d, s, b * 128 : (b + 1) * 128, c * 128 : (c + 1) * 128] = total.astype(BF)


def source_of(back):
    zl, zh, core = lax.axis_index("zl"), lax.axis_index("zh"), lax.axis_index("core")
    turn = jnp.int32(0)
    for i in range(2):
        for j in range(4):
            for k in range(2):
                here = jnp.logical_and(jnp.logical_and(zl == i, zh == j), core == k)
                turn = jnp.where(here, TURN[i][j][k], turn)
    return lax.rem(lax.axis_index("y") - lax.axis_index("x") + turn + 8 - back, 4)


def terms(d, mix, keys, parts):
    total = None
    for (back, half), part in zip(keys, parts):
        left = mix[d, source_of(back), :, half * 256 : (half + 1) * 256]
        term = jnp.dot(left, part[...], preferred_element_type=F32)
        total = term if total is None else total + term
    return total


def first_kernel(keys, mix, *refs):
    for d in range(2):
        refs[-1][d] = terms(d, mix, keys, refs[:-1])


def next_kernel(keys, mix, begun, *refs):
    for d in range(2):
        refs[-1][d] = begun[d] + terms(d, mix, keys, refs[:-1])


def last_kernel(keys, mix, begun, *refs):
    core = lax.axis_index("core")
    for d, at in enumerate((core, 1 - core)):
        total = (begun[d] + terms(d, mix, keys, refs[:-1])).astype(BF)
        for r in range(8):
            refs[-1][at, r] = total[r * 64 : (r + 1) * 64]


def layer_kernel(recv, weight, bias, cot, out, packed):
    halves = []
    for c in range(2):
        total = recv[8 * c].astype(F32)
        for r in range(1, 8):
            total = total + recv[8 * c + r].astype(F32)
        halves.append(total.astype(BF))
    mixed = jnp.concatenate(halves, axis=1)
    pre = jnp.dot(mixed, weight[...], preferred_element_type=F32) + bias[...]
    sig = jax.nn.sigmoid(pre)
    out[...] = (pre * sig).astype(BF)
    grad = cot[...].astype(F32) * sig * (1.0 + pre * (1.0 - sig))
    low = grad.astype(BF).astype(F32)
    wide = mixed.astype(F32)
    for i in range(4):
        part = wide[:, i * 192 : (i + 1) * 192]
        for j in range(4):
            both = jnp.concatenate([part, low[:, j * 192 : (j + 1) * 192]], axis=1)
            packed[i * 4 + j] = both.astype(BF)


def with_bias(block, row):
    high = row.astype(BF).astype(F32)
    low = row - high
    at = lax.broadcasted_iota(jnp.int32, (8, 384), 0)
    extra = jnp.where(at == 0, high, jnp.where(at == 1, low, 0.0))
    return jnp.concatenate([block, extra], axis=0)


def block_kernel(recv, keep, send):
    data = recv[...]
    left = data[:, :192]
    right = data[:, 192:]
    block = lax.dot_general(left, right, (((0,), (0,)), ((), ())), preferred_element_type=F32)
    row = jnp.sum(right.astype(F32), axis=0, keepdims=True)
    row = jnp.concatenate([row, row], axis=1)
    halves = [
        with_bias(
            jnp.concatenate([block[h * 96 : h * 96 + 48], block[h * 96 + 48 : h * 96 + 96]], axis=1),
            row,
        ).astype(BF)
        for h in range(2)
    ]
    first = lax.axis_index("core") == 0
    keep[...] = jnp.where(first, halves[0], halves[1])
    send[...] = jnp.where(first, halves[1], halves[0])


def resplit(total):
    row = total[48:49] + total[49:50]
    return with_bias(total[:48], row).astype(BF)


def four_kernel(copies, one, two, three, four, out):
    total = (one[...].astype(F32) + two[...].astype(F32)) + (three[...].astype(F32) + four[...].astype(F32))
    value = resplit(total)
    if copies is None:
        out[...] = value
    else:
        for i in range(copies):
            out[i] = value


def write_rows(source, at, grad, rows, sems):
    copies = []
    for i in range(4):
        pieces = [source[i * 4 + j].astype(F32) for j in range(4)]
        for h in range(2):
            rows[i, h * 48 : (h + 1) * 48] = jnp.concatenate(
                [piece[:48, h * 192 : (h + 1) * 192] for piece in pieces], axis=1
            )
        start = pl.multiple_of(i * 192 + at * 96, 32)
        copies.append(pltpu.make_async_copy(rows.at[i], grad.at[pl.ds(start, 96)], sems.at[i]))
        copies[-1].start()
    return copies


def own_half_kernel(own, grad, bias, rows, sems):
    copies = write_rows(own, lax.axis_index("core"), grad, rows, sems)
    parts = [own[j].astype(F32) for j in range(4)]
    bias[...] = jnp.concatenate([part[48:49, :192] + part[49:50, :192] for part in parts], axis=1)
    for copy in copies:
        copy.wait()


def other_half_kernel(other, begun, grad, rows, sems):
    del begun
    for copy in write_rows(other, 1 - lax.axis_index("core"), grad, rows, sems):
        copy.wait()


def neighbours(piece, step):
    return [lax.ppermute(piece, "zh", shift(4, step))] + [lax.ppermute(piece, "y", shift(4, k)) for k in BACK[1:]]


def product(kernel, keys, mix, parts, begun=None):
    last = kernel is last_kernel
    extra = [] if begun is None else [begun]
    return call(
        lambda *refs: kernel(keys, *refs),
        struct((2, 8, 64, 384), BF) if last else struct((2, 512, 384), F32),
        [vmem()] * (1 + len(extra) + len(parts)),
        vmem(),
        aliases={1: 0} if extra and not last else None,
        flops=4 * 512 * 256 * 384 * len(parts),
    )(mix, *extra, *parts)


def on_device(features, tiles, tile_cols, tile_mask, weight, bias, cotangent):
    with jax.named_scope("spread_features"):
        halves = call(
            pick_kernel,
            (struct((256, 384), BF), struct((256, 384), BF)),
            [hbm()],
            (vmem(), vmem()),
            [pltpu.SemaphoreType.DMA((2,))],
        )(features)
        *halves, tiles = lax.optimization_barrier((*halves, tiles))
        own = [lax.ppermute(half, AXES, first_hop()) for half in halves]
    with jax.named_scope("spread_tiles"):
        there = [lax.ppermute(value, "core", shift(2, 1)) for value in (tiles, tile_cols, tile_mask)]
        mix = call(
            spread_kernel,
            struct((2, 4, 512, 512), BF),
            [smem(), smem(), smem(), smem(), vmem(), vmem()],
            vmem(),
        )(tile_cols, tile_mask, *there[1:], tiles, there[0])
    own[0], mix, bias = lax.optimization_barrier((own[0], mix, bias.reshape(1, 768)))
    with jax.named_scope("spread_features"):
        early = neighbours(own[0], 3)
    with jax.named_scope("spread_features"):
        late = neighbours(own[1], 1)
    with jax.named_scope("aggregate"):
        begun = product(first_kernel, [(0, 0), (0, 1)], mix, own)
        begun = product(next_kernel, [(back, 0) for back in BACK], mix, early, begun)
        begun = product(next_kernel, [(BACK[0], 1)], mix, late[:1], begun)
        begun = product(next_kernel, [(BACK[1], 1)], mix, late[1:2], begun)
        partial = product(last_kernel, [(BACK[2], 1)], mix, late[2:], begun)
    with jax.named_scope("sum_over_rep"):
        recv = lax.all_to_all(partial.reshape(1024, 384), ("core",) + REP, 0, 0, tiled=True)
    with jax.named_scope("layer"):
        output, packed = call(
            layer_kernel,
            (struct((64, 768), BF), struct((16, 64, 384), BF)),
            [vmem()] * 4,
            (vmem(), vmem()),
        )(recv.reshape(16, 64, 384), weight, bias, cotangent)
    with jax.named_scope("exchange_rows"):
        rows = lax.all_to_all(packed.reshape(1024, 384), PLANE, 0, 0, tiled=True)
    with jax.named_scope("weight_block"):
        keep, send = call(
            block_kernel, (struct((56, 384), BF), struct((56, 384), BF)), [vmem()], (vmem(), vmem())
        )(rows)
        beside = lax.ppermute(keep, "zl", shift(2, 1))
        across = lax.ppermute(send, ("core", "zl"), [(0, 3), (1, 2), (2, 1), (3, 0)])
        other = lax.ppermute(send, "core", shift(2, 1))
        pair = call(
            lambda *refs: four_kernel(None, *refs), struct((56, 384), BF), [vmem()] * 4, vmem()
        )(keep, other, beside, across)
    with jax.named_scope("sum_over_z"):
        chain = [lax.ppermute(pair, "zh", shift(4, back)) for back in BACK]
        whole = call(
            lambda *refs: four_kernel(16, *refs), struct((16, 56, 384), BF), [vmem()] * 4, vmem()
        )(pair, *chain)
    with jax.named_scope("gather_plane"):
        mine = lax.all_to_all(whole.reshape(896, 384), PLANE, 0, 0, tiled=True)
        theirs = lax.ppermute(mine, "core", shift(2, 1))
    with jax.named_scope("finish"):
        scratch = [pltpu.VMEM((4, 96, 768), F32), pltpu.SemaphoreType.DMA((4,))]
        grad, grad_bias = call(
            own_half_kernel,
            (struct((768, 768), F32), struct((1, 768), F32)),
            [vmem()],
            (anyspace(), vmem()),
            scratch,
        )(mine.reshape(16, 56, 384))
        grad_weight = call(
            other_half_kernel,
            struct((768, 768), F32),
            [vmem(), anyspace()],
            anyspace(),
            scratch,
            aliases={1: 0},
        )(theirs.reshape(16, 56, 384), grad)
    return output, grad_weight, grad_bias.reshape(768)


def solution(mesh):
    fine = Mesh(mesh.devices.reshape(SIZES), AXES)
    placed = (
        P(DOM, None),
        P(DOM, REP, None, None, None),
        P(DOM, REP, None),
        P(DOM, REP, None),
        P(),
        P(),
        P(DOM + REP, None),
    )
    return jax.shard_map(
        on_device,
        mesh=fine,
        in_specs=placed,
        out_specs=(P(DOM + REP, None), P(), P()),
        check_vma=False,
    )
```

```python
import jax
import jax.numpy as jnp
import numpy as np
from jax import lax
from jax.experimental import pallas as pl
from jax.experimental.pallas import tpu as pltpu
from jax.sharding import Mesh, PartitionSpec as P

AXES = ("y", "zh", "core", "x", "zl")
SIZES = (4, 4, 2, 4, 2)
DOM = ("y", "zh", "core")
REP = ("x", "zl")
PLANE = ("x", "y")
BF = jnp.bfloat16
F32 = jnp.float32
BACK = (2, 1, 3)
VMEM_LIMIT = 32 * 1024 * 1024

TURN = (((1, 3), (3, 1), (1, 3), (3, 1)), ((1, 0), (3, 2), (1, 0), (3, 2)))
OFFSET = (
    ((3, 2, 0, 1), (1, 2, 3, 0), (3, 0, 1, 2), (0, 3, 1, 2), (1, 3, 2, 0), (2, 1, 0, 3), (2, 0, 3, 1), (0, 1, 2, 3)),
    ((0, 3, 1, 2), (2, 0, 3, 1), (2, 0, 1, 3), (0, 1, 2, 3), (1, 2, 3, 0), (3, 1, 0, 2), (3, 2, 0, 1), (1, 3, 2, 0)),
)


def first_hop():
    pairs = []
    for target in np.ndindex(*SIZES):
        y, zh, core, x, zl = target
        s = (y - x + TURN[zl][zh][core]) % 4
        source = (x, 2 * zl + s // 2, s % 2, (x + OFFSET[zl][2 * s + core][zh]) % 4, core)
        pairs.append((int(np.ravel_multi_index(source, SIZES)), int(np.ravel_multi_index(target, SIZES))))
    return sorted(pairs)


def shift(n, k):
    return [(i, (i + k) % n) for i in range(n)]


def vmem():
    return pl.BlockSpec(memory_space=pltpu.VMEM)


def smem():
    return pl.BlockSpec(memory_space=pltpu.SMEM)


def hbm():
    return pl.BlockSpec(memory_space=pltpu.HBM)


def anyspace():
    return pl.BlockSpec(memory_space=pl.ANY)


def struct(shape, dtype):
    return jax.ShapeDtypeStruct(shape, dtype)


def call(kernel, shapes, specs, out_specs, scratch=(), aliases=None, flops=0):
    return pl.pallas_call(
        kernel,
        out_shape=shapes,
        in_specs=specs,
        out_specs=out_specs,
        scratch_shapes=scratch,
        input_output_aliases=aliases or {},
        compiler_params=pltpu.CompilerParams(vmem_limit_bytes=VMEM_LIMIT),
        cost_estimate=pl.CostEstimate(flops=flops, bytes_accessed=1 << 20, transcendentals=0),
    )


def pick_kernel(features, one, two, sems):
    start = pl.multiple_of(lax.axis_index("zl") * 384, 384)
    copies = [
        pltpu.make_async_copy(features.at[pl.ds(i * 256, 256), pl.ds(start, 384)], out, sems.at[i])
        for i, out in enumerate((one, two))
    ]
    for copy in copies:
        copy.start()
    for copy in copies:
        copy.wait()


def spread_kernel(cols, live, other_cols, other_live, tiles, other_tiles, out):
    for d, (col, on, tile) in enumerate(((cols, live, tiles), (other_cols, other_live, other_tiles))):
        for b in range(4):
            for s in range(4):
                picks = [jnp.where(on[b, s, k] != 0, col[b, s, k], -1) for k in range(4)]
                parts = [tile[b, s, k].astype(F32) for k in range(4)]
                for c in range(4):
                    total = jnp.zeros((128, 128), F32)
                    for pick, part in zip(picks, parts):
                        total = total + jnp.where(pick == c, part, 0.0)
                    out[d, s, b * 128 : (b + 1) * 128, c * 128 : (c + 1) * 128] = total.astype(BF)


def source_of(back):
    zl, zh, core = lax.axis_index("zl"), lax.axis_index("zh"), lax.axis_index("core")
    turn = jnp.int32(0)
    for i in range(2):
        for j in range(4):
            for k in range(2):
                here = jnp.logical_and(jnp.logical_and(zl == i, zh == j), core == k)
                turn = jnp.where(here, TURN[i][j][k], turn)
    return lax.rem(lax.axis_index("y") - lax.axis_index("x") + turn + 8 - back, 4)


def terms(d, mix, keys, parts):
    total = None
    for (back, half), part in zip(keys, parts):
        left = mix[d, source_of(back), :, half * 256 : (half + 1) * 256]
        term = jnp.dot(left, part[...], preferred_element_type=F32)
        total = term if total is None else total + term
    return total


def first_kernel(keys, mix, *refs):
    for d in range(2):
        refs[-1][d] = terms(d, mix, keys, refs[:-1])


def next_kernel(keys, mix, begun, *refs):
    for d in range(2):
        refs[-1][d] = begun[d] + terms(d, mix, keys, refs[:-1])


def last_kernel(keys, mix, begun, *refs):
    core = lax.axis_index("core")
    for d, at in enumerate((core, 1 - core)):
        total = (begun[d] + terms(d, mix, keys, refs[:-1])).astype(BF)
        for r in range(8):
            refs[-1][at, r] = total[r * 64 : (r + 1) * 64]


def layer_kernel(recv, weight, bias, cot, out, packed):
    halves = []
    for c in range(2):
        total = recv[8 * c].astype(F32)
        for r in range(1, 8):
            total = total + recv[8 * c + r].astype(F32)
        halves.append(total.astype(BF))
    mixed = jnp.concatenate(halves, axis=1)
    pre = jnp.dot(mixed, weight[...], preferred_element_type=F32) + bias[...]
    sig = jax.nn.sigmoid(pre)
    out[...] = (pre * sig).astype(BF)
    grad = cot[...].astype(F32) * sig * (1.0 + pre * (1.0 - sig))
    low = grad.astype(BF).astype(F32)
    wide = mixed.astype(F32)
    for i in range(4):
        part = wide[:, i * 192 : (i + 1) * 192]
        for j in range(4):
            both = jnp.concatenate([part, low[:, j * 192 : (j + 1) * 192]], axis=1)
            packed[i * 4 + j] = both.astype(BF)


def with_bias(block, row):
    high = row.astype(BF).astype(F32)
    low = row - high
    at = lax.broadcasted_iota(jnp.int32, (8, 384), 0)
    extra = jnp.where(at == 0, high, jnp.where(at == 1, low, 0.0))
    return jnp.concatenate([block, extra], axis=0)


def block_kernel(recv, keep, send):
    data = recv[...]
    left = data[:, :192]
    right = data[:, 192:]
    block = lax.dot_general(left, right, (((0,), (0,)), ((), ())), preferred_element_type=F32)
    row = jnp.sum(right.astype(F32), axis=0, keepdims=True)
    row = jnp.concatenate([row, row], axis=1)
    halves = [
        with_bias(
            jnp.concatenate([block[h * 96 : h * 96 + 48], block[h * 96 + 48 : h * 96 + 96]], axis=1),
            row,
        ).astype(BF)
        for h in range(2)
    ]
    first = lax.axis_index("core") == 0
    keep[...] = jnp.where(first, halves[0], halves[1])
    send[...] = jnp.where(first, halves[1], halves[0])


def resplit(total):
    row = total[48:49] + total[49:50]
    return with_bias(total[:48], row).astype(BF)


def four_kernel(copies, one, two, three, four, out):
    total = (one[...].astype(F32) + two[...].astype(F32)) + (three[...].astype(F32) + four[...].astype(F32))
    value = resplit(total)
    if copies is None:
        out[...] = value
    else:
        for i in range(copies):
            out[i] = value


def write_rows(source, at, grad, rows, sems):
    copies = []
    for i in range(4):
        pieces = [source[i * 4 + j].astype(F32) for j in range(4)]
        for h in range(2):
            rows[i, h * 48 : (h + 1) * 48] = jnp.concatenate(
                [piece[:48, h * 192 : (h + 1) * 192] for piece in pieces], axis=1
            )
        start = pl.multiple_of(i * 192 + at * 96, 32)
        copies.append(pltpu.make_async_copy(rows.at[i], grad.at[pl.ds(start, 96)], sems.at[i]))
        copies[-1].start()
    return copies


def own_half_kernel(own, grad, bias, rows, sems):
    copies = write_rows(own, lax.axis_index("core"), grad, rows, sems)
    parts = [own[j].astype(F32) for j in range(4)]
    bias[...] = jnp.concatenate([part[48:49, :192] + part[49:50, :192] for part in parts], axis=1)
    for copy in copies:
        copy.wait()


def other_half_kernel(other, begun, grad, rows, sems):
    del begun
    for copy in write_rows(other, 1 - lax.axis_index("core"), grad, rows, sems):
        copy.wait()


def neighbours(piece, step):
    return [lax.ppermute(piece, "zh", shift(4, step))] + [lax.ppermute(piece, "y", shift(4, k)) for k in BACK[1:]]


def product(kernel, keys, mix, parts, begun=None):
    last = kernel is last_kernel
    extra = [] if begun is None else [begun]
    return call(
        lambda *refs: kernel(keys, *refs),
        struct((2, 8, 64, 384), BF) if last else struct((2, 512, 384), F32),
        [vmem()] * (1 + len(extra) + len(parts)),
        vmem(),
        aliases={1: 0} if extra and not last else None,
        flops=4 * 512 * 256 * 384 * len(parts),
    )(mix, *extra, *parts)


def on_device(features, tiles, tile_cols, tile_mask, weight, bias, cotangent):
    with jax.named_scope("spread_features"):
        halves = call(
            pick_kernel,
            (struct((256, 384), BF), struct((256, 384), BF)),
            [hbm()],
            (vmem(), vmem()),
            [pltpu.SemaphoreType.DMA((2,))],
        )(features)
        *halves, tiles = lax.optimization_barrier((*halves, tiles))
        own = [lax.ppermute(half, AXES, first_hop()) for half in halves]
    with jax.named_scope("spread_tiles"):
        there = [lax.ppermute(value, "core", shift(2, 1)) for value in (tiles, tile_cols, tile_mask)]
        mix = call(
            spread_kernel,
            struct((2, 4, 512, 512), BF),
            [smem(), smem(), smem(), smem(), vmem(), vmem()],
            vmem(),
        )(tile_cols, tile_mask, *there[1:], tiles, there[0])
    own[0], mix = lax.optimization_barrier((own[0], mix))
    with jax.named_scope("spread_features"):
        early = neighbours(own[0], 3)
    with jax.named_scope("spread_features"):
        late = neighbours(own[1], 1)
    with jax.named_scope("aggregate"):
        begun = product(first_kernel, [(0, 0), (0, 1)], mix, own)
        begun = product(next_kernel, [(back, 0) for back in BACK], mix, early, begun)
        begun = product(next_kernel, [(BACK[0], 1)], mix, late[:1], begun)
        begun = product(next_kernel, [(BACK[1], 1)], mix, late[1:2], begun)
        partial = product(last_kernel, [(BACK[2], 1)], mix, late[2:], begun)
    with jax.named_scope("sum_over_rep"):
        recv = lax.all_to_all(partial.reshape(1024, 384), ("core",) + REP, 0, 0, tiled=True)
    with jax.named_scope("layer"):
        output, packed = call(
            layer_kernel,
            (struct((64, 768), BF), struct((16, 64, 384), BF)),
            [vmem()] * 4,
            (vmem(), vmem()),
        )(recv.reshape(16, 64, 384), weight, bias.reshape(1, 768), cotangent)
    with jax.named_scope("exchange_rows"):
        rows = lax.all_to_all(packed.reshape(1024, 384), PLANE, 0, 0, tiled=True)
    with jax.named_scope("weight_block"):
        keep, send = call(
            block_kernel, (struct((56, 384), BF), struct((56, 384), BF)), [vmem()], (vmem(), vmem())
        )(rows)
        beside = lax.ppermute(keep, "zl", shift(2, 1))
        across = lax.ppermute(send, ("core", "zl"), [(0, 3), (1, 2), (2, 1), (3, 0)])
        other = lax.ppermute(send, "core", shift(2, 1))
        pair = call(
            lambda *refs: four_kernel(None, *refs), struct((56, 384), BF), [vmem()] * 4, vmem()
        )(keep, other, beside, across)
    with jax.named_scope("sum_over_z"):
        chain = [lax.ppermute(pair, "zh", shift(4, back)) for back in BACK]
        whole = call(
            lambda *refs: four_kernel(16, *refs), struct((16, 56, 384), BF), [vmem()] * 4, vmem()
        )(pair, *chain)
    with jax.named_scope("gather_plane"):
        mine = lax.all_to_all(whole.reshape(896, 384), PLANE, 0, 0, tiled=True)
        theirs = lax.ppermute(mine, "core", shift(2, 1))
    with jax.named_scope("finish"):
        scratch = [pltpu.VMEM((4, 96, 768), F32), pltpu.SemaphoreType.DMA((4,))]
        grad, grad_bias = call(
            own_half_kernel,
            (struct((768, 768), F32), struct((1, 768), F32)),
            [vmem()],
            (anyspace(), vmem()),
            scratch,
        )(mine.reshape(16, 56, 384))
        grad_weight = call(
            other_half_kernel,
            struct((768, 768), F32),
            [vmem(), anyspace()],
            anyspace(),
            scratch,
            aliases={1: 0},
        )(theirs.reshape(16, 56, 384), grad)
    return output, grad_weight, grad_bias.reshape(768)


def solution(mesh):
    fine = Mesh(mesh.devices.reshape(SIZES), AXES)
    placed = (
        P(DOM, None),
        P(DOM, REP, None, None, None),
        P(DOM, REP, None),
        P(DOM, REP, None),
        P(),
        P(),
        P(DOM + REP, None),
    )
    return jax.shard_map(
        on_device,
        mesh=fine,
        in_specs=placed,
        out_specs=(P(DOM + REP, None), P(), P()),
        check_vma=False,
    )
```

```python
import jax
import jax.numpy as jnp
import numpy as np
from jax import lax
from jax.experimental import pallas as pl
from jax.experimental.pallas import tpu as pltpu
from jax.sharding import Mesh, PartitionSpec as P

AXES = ("y", "zh", "core", "x", "zl")
SIZES = (4, 4, 2, 4, 2)
DOM = ("y", "zh", "core")
REP = ("x", "zl")
PLANE = ("x", "y")
BF = jnp.bfloat16
F32 = jnp.float32
BACK = (2, 1, 3)
VMEM_LIMIT = 32 * 1024 * 1024

TURN = (((1, 0), (3, 2), (1, 0), (3, 2)), ((2, 0), (0, 2), (2, 0), (0, 2)))
OFFSET = (
    ((3, 2, 0, 1), (2, 0, 1, 3), (0, 2, 3, 1), (1, 3, 2, 0), (2, 0, 1, 3), (0, 1, 3, 2), (1, 3, 0, 2), (3, 1, 2, 0)),
    ((3, 2, 0, 1), (2, 1, 3, 0), (1, 2, 0, 3), (3, 0, 2, 1), (1, 0, 2, 3), (3, 1, 0, 2), (1, 3, 2, 0), (0, 3, 1, 2)),
)


def first_hop():
    pairs = []
    for target in np.ndindex(*SIZES):
        y, zh, core, x, zl = target
        s = (y - x + TURN[zl][zh][core]) % 4
        source = (x, 2 * zl + s // 2, s % 2, (x + OFFSET[zl][2 * s + core][zh]) % 4, core)
        pairs.append((int(np.ravel_multi_index(source, SIZES)), int(np.ravel_multi_index(target, SIZES))))
    return sorted(pairs)


def shift(n, k):
    return [(i, (i + k) % n) for i in range(n)]


def vmem():
    return pl.BlockSpec(memory_space=pltpu.VMEM)


def smem():
    return pl.BlockSpec(memory_space=pltpu.SMEM)


def hbm():
    return pl.BlockSpec(memory_space=pltpu.HBM)


def anyspace():
    return pl.BlockSpec(memory_space=pl.ANY)


def struct(shape, dtype):
    return jax.ShapeDtypeStruct(shape, dtype)


def call(kernel, shapes, specs, out_specs, scratch=(), aliases=None, flops=0):
    return pl.pallas_call(
        kernel,
        out_shape=shapes,
        in_specs=specs,
        out_specs=out_specs,
        scratch_shapes=scratch,
        input_output_aliases=aliases or {},
        compiler_params=pltpu.CompilerParams(vmem_limit_bytes=VMEM_LIMIT),
        cost_estimate=pl.CostEstimate(flops=flops, bytes_accessed=1 << 20, transcendentals=0),
    )


def pick_kernel(features, one, two, sems):
    start = pl.multiple_of(lax.axis_index("zl") * 384, 384)
    copies = [
        pltpu.make_async_copy(features.at[pl.ds(i * 256, 256), pl.ds(start, 384)], out, sems.at[i])
        for i, out in enumerate((one, two))
    ]
    for copy in copies:
        copy.start()
    for copy in copies:
        copy.wait()


def spread_kernel(cols, live, other_cols, other_live, tiles, other_tiles, out):
    for d, (col, on, tile) in enumerate(((cols, live, tiles), (other_cols, other_live, other_tiles))):
        for b in range(4):
            for s in range(4):
                picks = [jnp.where(on[b, s, k] != 0, col[b, s, k], -1) for k in range(4)]
                parts = [tile[b, s, k].astype(F32) for k in range(4)]
                for c in range(4):
                    total = jnp.zeros((128, 128), F32)
                    for pick, part in zip(picks, parts):
                        total = total + jnp.where(pick == c, part, 0.0)
                    out[d, s, b * 128 : (b + 1) * 128, c * 128 : (c + 1) * 128] = total.astype(BF)


def source_of(back):
    zl, zh, core = lax.axis_index("zl"), lax.axis_index("zh"), lax.axis_index("core")
    turn = jnp.int32(0)
    for i in range(2):
        for j in range(4):
            for k in range(2):
                here = jnp.logical_and(jnp.logical_and(zl == i, zh == j), core == k)
                turn = jnp.where(here, TURN[i][j][k], turn)
    return lax.rem(lax.axis_index("y") - lax.axis_index("x") + turn + 8 - back, 4)


def terms(d, mix, keys, parts):
    total = None
    for (back, half), part in zip(keys, parts):
        left = mix[d, source_of(back), :, half * 256 : (half + 1) * 256]
        term = jnp.dot(left, part[...], preferred_element_type=F32)
        total = term if total is None else total + term
    return total


def first_kernel(keys, mix, *refs):
    for d in range(2):
        refs[-1][d] = terms(d, mix, keys, refs[:-1])


def next_kernel(keys, mix, begun, *refs):
    for d in range(2):
        refs[-1][d] = begun[d] + terms(d, mix, keys, refs[:-1])


def last_kernel(keys, mix, begun, *refs):
    core = lax.axis_index("core")
    for d, at in enumerate((core, 1 - core)):
        total = (begun[d] + terms(d, mix, keys, refs[:-1])).astype(BF)
        for r in range(8):
            refs[-1][at, r] = total[r * 64 : (r + 1) * 64]


def layer_kernel(recv, weight, bias, cot, out, packed):
    halves = []
    for c in range(2):
        total = recv[8 * c].astype(F32)
        for r in range(1, 8):
            total = total + recv[8 * c + r].astype(F32)
        halves.append(total.astype(BF))
    mixed = jnp.concatenate(halves, axis=1)
    pre = jnp.dot(mixed, weight[...], preferred_element_type=F32) + bias[...]
    sig = jax.nn.sigmoid(pre)
    out[...] = (pre * sig).astype(BF)
    grad = cot[...].astype(F32) * sig * (1.0 + pre * (1.0 - sig))
    low = grad.astype(BF).astype(F32)
    wide = mixed.astype(F32)
    for i in range(4):
        part = wide[:, i * 192 : (i + 1) * 192]
        for j in range(4):
            both = jnp.concatenate([part, low[:, j * 192 : (j + 1) * 192]], axis=1)
            packed[i * 4 + j] = both.astype(BF)


def with_bias(block, row):
    high = row.astype(BF).astype(F32)
    low = row - high
    at = lax.broadcasted_iota(jnp.int32, (8, 384), 0)
    extra = jnp.where(at == 0, high, jnp.where(at == 1, low, 0.0))
    return jnp.concatenate([block, extra], axis=0)


def block_kernel(recv, keep, send):
    data = recv[...]
    left = data[:, :192]
    right = data[:, 192:]
    block = lax.dot_general(left, right, (((0,), (0,)), ((), ())), preferred_element_type=F32)
    row = jnp.sum(right.astype(F32), axis=0, keepdims=True)
    row = jnp.concatenate([row, row], axis=1)
    halves = [
        with_bias(
            jnp.concatenate([block[h * 96 : h * 96 + 48], block[h * 96 + 48 : h * 96 + 96]], axis=1),
            row,
        ).astype(BF)
        for h in range(2)
    ]
    first = lax.axis_index("core") == 0
    keep[...] = jnp.where(first, halves[0], halves[1])
    send[...] = jnp.where(first, halves[1], halves[0])


def resplit(total):
    row = total[48:49] + total[49:50]
    return with_bias(total[:48], row).astype(BF)


def four_kernel(copies, one, two, three, four, out):
    total = (one[...].astype(F32) + two[...].astype(F32)) + (three[...].astype(F32) + four[...].astype(F32))
    value = resplit(total)
    if copies is None:
        out[...] = value
    else:
        for i in range(copies):
            out[i] = value


def write_rows(source, at, grad, rows, sems):
    copies = []
    for i in range(4):
        pieces = [source[i * 4 + j].astype(F32) for j in range(4)]
        for h in range(2):
            rows[i, h * 48 : (h + 1) * 48] = jnp.concatenate(
                [piece[:48, h * 192 : (h + 1) * 192] for piece in pieces], axis=1
            )
        start = pl.multiple_of(i * 192 + at * 96, 32)
        copies.append(pltpu.make_async_copy(rows.at[i], grad.at[pl.ds(start, 96)], sems.at[i]))
        copies[-1].start()
    return copies


def own_half_kernel(own, grad, bias, rows, sems):
    copies = write_rows(own, lax.axis_index("core"), grad, rows, sems)
    parts = [own[j].astype(F32) for j in range(4)]
    bias[...] = jnp.concatenate([part[48:49, :192] + part[49:50, :192] for part in parts], axis=1)
    for copy in copies:
        copy.wait()


def other_half_kernel(other, begun, grad, rows, sems):
    del begun
    for copy in write_rows(other, 1 - lax.axis_index("core"), grad, rows, sems):
        copy.wait()


def neighbours(piece, step):
    return [lax.ppermute(piece, "zh", shift(4, step))] + [lax.ppermute(piece, "y", shift(4, k)) for k in BACK[1:]]


def product(kernel, keys, mix, parts, begun=None):
    last = kernel is last_kernel
    extra = [] if begun is None else [begun]
    return call(
        lambda *refs: kernel(keys, *refs),
        struct((2, 8, 64, 384), BF) if last else struct((2, 512, 384), F32),
        [vmem()] * (1 + len(extra) + len(parts)),
        vmem(),
        aliases={1: 0} if extra and not last else None,
        flops=4 * 512 * 256 * 384 * len(parts),
    )(mix, *extra, *parts)


def on_device(features, tiles, tile_cols, tile_mask, weight, bias, cotangent):
    with jax.named_scope("spread_features"):
        halves = call(
            pick_kernel,
            (struct((256, 384), BF), struct((256, 384), BF)),
            [hbm()],
            (vmem(), vmem()),
            [pltpu.SemaphoreType.DMA((2,))],
        )(features)
        *halves, tiles = lax.optimization_barrier((*halves, tiles))
        own = [lax.ppermute(half, AXES, first_hop()) for half in halves]
    with jax.named_scope("spread_tiles"):
        there = [lax.ppermute(value, "core", shift(2, 1)) for value in (tiles, tile_cols, tile_mask)]
        mix = call(
            spread_kernel,
            struct((2, 4, 512, 512), BF),
            [smem(), smem(), smem(), smem(), vmem(), vmem()],
            vmem(),
        )(tile_cols, tile_mask, *there[1:], tiles, there[0])
    own[0], mix = lax.optimization_barrier((own[0], mix))
    with jax.named_scope("spread_features"):
        early = neighbours(own[0], 3)
    with jax.named_scope("spread_features"):
        late = neighbours(own[1], 1)
    with jax.named_scope("aggregate"):
        begun = product(first_kernel, [(0, 0), (0, 1)], mix, own)
        begun = product(next_kernel, [(back, 0) for back in BACK], mix, early, begun)
        begun = product(next_kernel, [(BACK[0], 1)], mix, late[:1], begun)
        begun = product(next_kernel, [(BACK[1], 1)], mix, late[1:2], begun)
        partial = product(last_kernel, [(BACK[2], 1)], mix, late[2:], begun)
    with jax.named_scope("sum_over_rep"):
        recv = lax.all_to_all(partial.reshape(1024, 384), ("core",) + REP, 0, 0, tiled=True)
    with jax.named_scope("layer"):
        output, packed = call(
            layer_kernel,
            (struct((64, 768), BF), struct((16, 64, 384), BF)),
            [vmem()] * 4,
            (vmem(), vmem()),
        )(recv.reshape(16, 64, 384), weight, bias.reshape(1, 768), cotangent)
    with jax.named_scope("exchange_rows"):
        rows = lax.all_to_all(packed.reshape(1024, 384), PLANE, 0, 0, tiled=True)
    with jax.named_scope("weight_block"):
        keep, send = call(
            block_kernel, (struct((56, 384), BF), struct((56, 384), BF)), [vmem()], (vmem(), vmem())
        )(rows)
        beside = lax.ppermute(keep, "zl", shift(2, 1))
        across = lax.ppermute(send, ("core", "zl"), [(0, 3), (1, 2), (2, 1), (3, 0)])
        other = lax.ppermute(send, "core", shift(2, 1))
        pair = call(
            lambda *refs: four_kernel(None, *refs), struct((56, 384), BF), [vmem()] * 4, vmem()
        )(keep, other, beside, across)
    with jax.named_scope("sum_over_z"):
        chain = [lax.ppermute(pair, "zh", shift(4, back)) for back in BACK]
        whole = call(
            lambda *refs: four_kernel(16, *refs), struct((16, 56, 384), BF), [vmem()] * 4, vmem()
        )(pair, *chain)
    with jax.named_scope("gather_plane"):
        mine = lax.all_to_all(whole.reshape(896, 384), PLANE, 0, 0, tiled=True)
        theirs = lax.ppermute(mine, "core", shift(2, 1))
    with jax.named_scope("finish"):
        scratch = [pltpu.VMEM((4, 96, 768), F32), pltpu.SemaphoreType.DMA((4,))]
        grad, grad_bias = call(
            own_half_kernel,
            (struct((768, 768), F32), struct((1, 768), F32)),
            [vmem()],
            (anyspace(), vmem()),
            scratch,
        )(mine.reshape(16, 56, 384))
        grad_weight = call(
            other_half_kernel,
            struct((768, 768), F32),
            [vmem(), anyspace()],
            anyspace(),
            scratch,
            aliases={1: 0},
        )(theirs.reshape(16, 56, 384), grad)
    return output, grad_weight, grad_bias.reshape(768)


def solution(mesh):
    fine = Mesh(mesh.devices.reshape(SIZES), AXES)
    placed = (
        P(DOM, None),
        P(DOM, REP, None, None, None),
        P(DOM, REP, None),
        P(DOM, REP, None),
        P(),
        P(),
        P(DOM + REP, None),
    )
    return jax.shard_map(
        on_device,
        mesh=fine,
        in_specs=placed,
        out_specs=(P(DOM + REP, None), P(), P()),
        check_vma=False,
    )
```

```python
import jax
import jax.numpy as jnp
import numpy as np
from jax import lax
from jax.experimental import pallas as pl
from jax.experimental.pallas import tpu as pltpu
from jax.sharding import Mesh, PartitionSpec as P

AXES = ("y", "zh", "core", "x", "zl")
SIZES = (4, 4, 2, 4, 2)
DOM = ("y", "zh", "core")
REP = ("x", "zl")
PLANE = ("x", "y")
BF = jnp.bfloat16
F32 = jnp.float32
BACK = (2, 1, 3)
VMEM_LIMIT = 32 * 1024 * 1024

TURN = (((1, 0), (3, 2), (1, 0), (3, 2)), ((2, 0), (0, 2), (2, 0), (0, 2)))
OFFSET = (
    ((3, 2, 0, 1), (2, 0, 1, 3), (0, 2, 3, 1), (1, 3, 2, 0), (2, 0, 1, 3), (0, 1, 3, 2), (1, 3, 0, 2), (3, 1, 2, 0)),
    ((3, 2, 0, 1), (2, 1, 3, 0), (1, 2, 0, 3), (3, 0, 2, 1), (1, 0, 2, 3), (3, 1, 0, 2), (1, 3, 2, 0), (0, 3, 1, 2)),
)


def first_hop():
    pairs = []
    for target in np.ndindex(*SIZES):
        y, zh, core, x, zl = target
        s = (y - x + TURN[zl][zh][core]) % 4
        source = (x, 2 * zl + s // 2, s % 2, (x + OFFSET[zl][2 * s + core][zh]) % 4, core)
        pairs.append((int(np.ravel_multi_index(source, SIZES)), int(np.ravel_multi_index(target, SIZES))))
    return sorted(pairs)


def shift(n, k):
    return [(i, (i + k) % n) for i in range(n)]


def vmem():
    return pl.BlockSpec(memory_space=pltpu.VMEM)


def smem():
    return pl.BlockSpec(memory_space=pltpu.SMEM)


def hbm():
    return pl.BlockSpec(memory_space=pltpu.HBM)


def anyspace():
    return pl.BlockSpec(memory_space=pl.ANY)


def struct(shape, dtype):
    return jax.ShapeDtypeStruct(shape, dtype)


def call(kernel, shapes, specs, out_specs, scratch=(), aliases=None, flops=0):
    return pl.pallas_call(
        kernel,
        out_shape=shapes,
        in_specs=specs,
        out_specs=out_specs,
        scratch_shapes=scratch,
        input_output_aliases=aliases or {},
        compiler_params=pltpu.CompilerParams(vmem_limit_bytes=VMEM_LIMIT),
        cost_estimate=pl.CostEstimate(flops=flops, bytes_accessed=1 << 20, transcendentals=0),
    )


def pick_kernel(features, one, two, sems):
    start = pl.multiple_of(lax.axis_index("zl") * 384, 384)
    copies = [
        pltpu.make_async_copy(features.at[pl.ds(i * 256, 256), pl.ds(start, 384)], out, sems.at[i])
        for i, out in enumerate((one, two))
    ]
    for copy in copies:
        copy.start()
    for copy in copies:
        copy.wait()


def spread_kernel(cols, live, other_cols, other_live, tiles, other_tiles, out):
    for d, (col, on, tile) in enumerate(((cols, live, tiles), (other_cols, other_live, other_tiles))):
        for b in range(4):
            for s in range(4):
                picks = [jnp.where(on[b, s, k] != 0, col[b, s, k], -1) for k in range(4)]
                parts = [tile[b, s, k].astype(F32) for k in range(4)]
                for c in range(4):
                    total = jnp.zeros((128, 128), F32)
                    for pick, part in zip(picks, parts):
                        total = total + jnp.where(pick == c, part, 0.0)
                    out[d, s, b * 128 : (b + 1) * 128, c * 128 : (c + 1) * 128] = total.astype(BF)


def source_of(back):
    zl, zh, core = lax.axis_index("zl"), lax.axis_index("zh"), lax.axis_index("core")
    turn = jnp.int32(0)
    for i in range(2):
        for j in range(4):
            for k in range(2):
                here = jnp.logical_and(jnp.logical_and(zl == i, zh == j), core == k)
                turn = jnp.where(here, TURN[i][j][k], turn)
    return lax.rem(lax.axis_index("y") - lax.axis_index("x") + turn + 8 - back, 4)


def terms(d, mix, keys, parts):
    total = None
    for (back, half), part in zip(keys, parts):
        left = mix[d, source_of(back), :, half * 256 : (half + 1) * 256]
        term = jnp.dot(left, part[...], preferred_element_type=F32)
        total = term if total is None else total + term
    return total


def first_kernel(keys, mix, *refs):
    for d in range(2):
        refs[-1][d] = terms(d, mix, keys, refs[:-1])


def next_kernel(keys, mix, begun, *refs):
    for d in range(2):
        refs[-1][d] = begun[d] + terms(d, mix, keys, refs[:-1])


def last_kernel(keys, mix, begun, *refs):
    core = lax.axis_index("core")
    for d, at in enumerate((core, 1 - core)):
        total = (begun[d] + terms(d, mix, keys, refs[:-1])).astype(BF)
        for r in range(8):
            refs[-1][r, at] = total[r * 64 : (r + 1) * 64]


def rows_kernel(recv, out):
    total = recv[0].astype(F32)
    for r in range(1, 8):
        total = total + recv[r].astype(F32)
    out[...] = total.astype(BF)


def with_bias(block, row):
    high = row.astype(BF).astype(F32)
    low = row - high
    at = lax.broadcasted_iota(jnp.int32, (8, 384), 0)
    extra = jnp.where(at == 0, high, jnp.where(at == 1, low, 0.0))
    return jnp.concatenate([block, extra], axis=0).astype(BF)


def layer_kernel(mine, other, weight, bias, cot, other_cot, out, packed):
    first = lax.axis_index("core") == 0
    left = jnp.where(first, mine[...], other[...]).reshape(128, 384)
    right = jnp.where(first, other[...], mine[...]).reshape(128, 384)
    mixed = jnp.concatenate([left, right], axis=1)
    pre = jnp.dot(mixed, weight[...], preferred_element_type=F32) + bias[...]
    sig = jax.nn.sigmoid(pre)
    act = pre * sig
    out[...] = jnp.where(first, act[:64], act[64:]).astype(BF)
    both = jnp.concatenate(
        [jnp.where(first, cot[...], other_cot[...]), jnp.where(first, other_cot[...], cot[...])], axis=0
    )
    grad = both.astype(F32) * sig * (1.0 + pre * (1.0 - sig))
    low = jnp.where(first, grad[:, :384], grad[:, 384:]).astype(BF)
    block = lax.dot_general(mixed, low, (((0,), (0,)), ((), ())), preferred_element_type=F32)
    row = jnp.sum(low.astype(F32), axis=0, keepdims=True)
    for i in range(16):
        packed[i] = with_bias(block[i * 48 : (i + 1) * 48], row)


def resplit(total):
    return with_bias(total[:48], total[48:49] + total[49:50])


def plane_kernel(recv, out):
    total = recv[0].astype(F32)
    for r in range(1, 16):
        total = total + recv[r].astype(F32)
    out[...] = resplit(total)


def pair_kernel(one, two, out):
    out[...] = resplit(one[...].astype(F32) + two[...].astype(F32))


def four_kernel(copies, one, two, three, four, out):
    total = (one[...].astype(F32) + two[...].astype(F32)) + (three[...].astype(F32) + four[...].astype(F32))
    value = resplit(total)
    for i in range(copies):
        out[i] = value


def write_columns(source, at, grad, rows, sems):
    start = pl.multiple_of(at * 384, 384)
    copies = []
    for i in range(4):
        for j in range(4):
            rows[i, j * 48 : (j + 1) * 48] = source[i * 4 + j].astype(F32)[:48]
        copies.append(
            pltpu.make_async_copy(rows.at[i], grad.at[pl.ds(i * 192, 192), pl.ds(start, 384)], sems.at[i])
        )
        copies[-1].start()
    return copies


def own_half_kernel(own, grad, rows, sems):
    for copy in write_columns(own, lax.axis_index("core"), grad, rows, sems):
        copy.wait()


def other_half_kernel(own, other, begun, grad, bias, rows, sems):
    del begun
    copies = write_columns(other, 1 - lax.axis_index("core"), grad, rows, sems)
    first = lax.axis_index("core") == 0
    mine, theirs = own[0].astype(F32), other[0].astype(F32)
    mine = mine[48:49] + mine[49:50]
    theirs = theirs[48:49] + theirs[49:50]
    row = jnp.concatenate([jnp.where(first, mine, theirs), jnp.where(first, theirs, mine)], axis=1)
    bias[...] = row.reshape(768)
    for copy in copies:
        copy.wait()


def neighbours(piece, step):
    return [lax.ppermute(piece, "zh", shift(4, step))] + [lax.ppermute(piece, "y", shift(4, k)) for k in BACK[1:]]


def product(kernel, keys, mix, parts, begun=None):
    last = kernel is last_kernel
    extra = [] if begun is None else [begun]
    return call(
        lambda *refs: kernel(keys, *refs),
        struct((8, 2, 64, 384), BF) if last else struct((2, 512, 384), F32),
        [vmem()] * (1 + len(extra) + len(parts)),
        vmem(),
        aliases={1: 0} if extra and not last else None,
        flops=4 * 512 * 256 * 384 * len(parts),
    )(mix, *extra, *parts)


def on_device(features, tiles, tile_cols, tile_mask, weight, bias, cotangent):
    with jax.named_scope("spread_features"):
        halves = call(
            pick_kernel,
            (struct((256, 384), BF), struct((256, 384), BF)),
            [hbm()],
            (vmem(), vmem()),
            [pltpu.SemaphoreType.DMA((2,))],
        )(features)
        *halves, tiles = lax.optimization_barrier((*halves, tiles))
        own = [lax.ppermute(half, AXES, first_hop()) for half in halves]
    with jax.named_scope("spread_tiles"):
        there = [lax.ppermute(value, "core", shift(2, 1)) for value in (tiles, tile_cols, tile_mask)]
        other_cot = lax.ppermute(cotangent, "core", shift(2, 1))
        mix = call(
            spread_kernel,
            struct((2, 4, 512, 512), BF),
            [smem(), smem(), smem(), smem(), vmem(), vmem()],
            vmem(),
        )(tile_cols, tile_mask, *there[1:], tiles, there[0])
    own[0], mix, other_cot = lax.optimization_barrier((own[0], mix, other_cot))
    with jax.named_scope("spread_features"):
        early = neighbours(own[0], 3)
    with jax.named_scope("spread_features"):
        late = neighbours(own[1], 1)
    with jax.named_scope("aggregate"):
        begun = product(first_kernel, [(0, 0), (0, 1)], mix, own)
        begun = product(next_kernel, [(back, 0) for back in BACK], mix, early, begun)
        begun = product(next_kernel, [(BACK[0], 1)], mix, late[:1], begun)
        begun = product(next_kernel, [(BACK[1], 1)], mix, late[1:2], begun)
        partial = product(last_kernel, [(BACK[2], 1)], mix, late[2:], begun)
    with jax.named_scope("sum_over_rep"):
        recv = lax.all_to_all(partial, REP, 0, 0, tiled=True)
        mixed = call(rows_kernel, struct((2, 64, 384), BF), [vmem()], vmem())(recv)
        other_mixed = lax.ppermute(mixed, "core", shift(2, 1))
    with jax.named_scope("layer"):
        output, packed = call(
            layer_kernel,
            (struct((64, 768), BF), struct((16, 56, 384), BF)),
            [vmem()] * 6,
            (vmem(), vmem()),
        )(mixed, other_mixed, weight, bias.reshape(1, 768), cotangent, other_cot)
    with jax.named_scope("sum_over_plane"):
        recv = lax.all_to_all(packed.reshape(896, 384), PLANE, 0, 0, tiled=True)
        part = call(plane_kernel, struct((56, 384), BF), [vmem()], vmem())(recv.reshape(16, 56, 384))
    with jax.named_scope("sum_over_z"):
        beside = lax.ppermute(part, "zl", shift(2, 1))
        part = call(pair_kernel, struct((56, 384), BF), [vmem()] * 2, vmem())(part, beside)
        chain = [lax.ppermute(part, "zh", shift(4, back)) for back in BACK]
        whole = call(
            lambda *refs: four_kernel(16, *refs), struct((16, 56, 384), BF), [vmem()] * 4, vmem()
        )(part, *chain)
    with jax.named_scope("gather_plane"):
        mine = lax.all_to_all(whole.reshape(896, 384), PLANE, 0, 0, tiled=True)
        theirs = lax.ppermute(mine, "core", shift(2, 1)).reshape(16, 56, 384)
        mine = mine.reshape(16, 56, 384)
    with jax.named_scope("finish"):
        scratch = [pltpu.VMEM((4, 192, 384), F32), pltpu.SemaphoreType.DMA((4,))]
        grad = call(own_half_kernel, struct((768, 768), F32), [vmem()], anyspace(), scratch)(mine)
        grad_weight, grad_bias = call(
            other_half_kernel,
            (struct((768, 768), F32), struct((768,), F32)),
            [vmem(), vmem(), anyspace()],
            (anyspace(), vmem()),
            scratch,
            aliases={2: 0},
        )(mine, theirs, grad)
    return output, grad_weight, grad_bias


def solution(mesh):
    fine = Mesh(mesh.devices.reshape(SIZES), AXES)
    placed = (
        P(DOM, None),
        P(DOM, REP, None, None, None),
        P(DOM, REP, None),
        P(DOM, REP, None),
        P(),
        P(),
        P(DOM + REP, None),
    )
    return jax.shard_map(
        on_device,
        mesh=fine,
        in_specs=placed,
        out_specs=(P(DOM + REP, None), P(), P()),
        check_vma=False,
    )
```

```python
import jax
import jax.numpy as jnp
import numpy as np
from jax import lax
from jax.experimental import pallas as pl
from jax.experimental.pallas import tpu as pltpu
from jax.sharding import Mesh, PartitionSpec as P

AXES = ("y", "zh", "core", "x", "zl")
SIZES = (4, 4, 2, 4, 2)
DOM = ("y", "zh", "core")
REP = ("x", "zl")
PLANE = ("x", "y")
BF = jnp.bfloat16
F32 = jnp.float32
BACK = (2, 1, 3)
VMEM_LIMIT = 32 * 1024 * 1024

TURN = (((1, 0), (3, 2), (1, 0), (3, 2)), ((2, 0), (0, 2), (2, 0), (0, 2)))
OFFSET = (
    ((3, 2, 0, 1), (2, 0, 1, 3), (0, 2, 3, 1), (1, 3, 2, 0), (2, 0, 1, 3), (0, 1, 3, 2), (1, 3, 0, 2), (3, 1, 2, 0)),
    ((3, 2, 0, 1), (2, 1, 3, 0), (1, 2, 0, 3), (3, 0, 2, 1), (1, 0, 2, 3), (3, 1, 0, 2), (1, 3, 2, 0), (0, 3, 1, 2)),
)


def first_hop():
    pairs = []
    for target in np.ndindex(*SIZES):
        y, zh, core, x, zl = target
        s = (y - x + TURN[zl][zh][core]) % 4
        source = (x, 2 * zl + s // 2, s % 2, (x + OFFSET[zl][2 * s + core][zh]) % 4, core)
        pairs.append((int(np.ravel_multi_index(source, SIZES)), int(np.ravel_multi_index(target, SIZES))))
    return sorted(pairs)


def shift(n, k):
    return [(i, (i + k) % n) for i in range(n)]


def vmem():
    return pl.BlockSpec(memory_space=pltpu.VMEM)


def smem():
    return pl.BlockSpec(memory_space=pltpu.SMEM)


def hbm():
    return pl.BlockSpec(memory_space=pltpu.HBM)


def anyspace():
    return pl.BlockSpec(memory_space=pl.ANY)


def struct(shape, dtype):
    return jax.ShapeDtypeStruct(shape, dtype)


def call(kernel, shapes, specs, out_specs, scratch=(), aliases=None, flops=0):
    return pl.pallas_call(
        kernel,
        out_shape=shapes,
        in_specs=specs,
        out_specs=out_specs,
        scratch_shapes=scratch,
        input_output_aliases=aliases or {},
        compiler_params=pltpu.CompilerParams(vmem_limit_bytes=VMEM_LIMIT),
        cost_estimate=pl.CostEstimate(flops=flops, bytes_accessed=1 << 20, transcendentals=0),
    )


def pick_kernel(features, one, two, sems):
    start = pl.multiple_of(lax.axis_index("zl") * 384, 384)
    copies = [
        pltpu.make_async_copy(features.at[pl.ds(i * 256, 256), pl.ds(start, 384)], out, sems.at[i])
        for i, out in enumerate((one, two))
    ]
    for copy in copies:
        copy.start()
    for copy in copies:
        copy.wait()


def spread_kernel(picks, other_picks, tiles, other_tiles, out):
    for d, (pick, tile) in enumerate(((picks, tiles), (other_picks, other_tiles))):
        for b in range(4):
            for s in range(4):
                parts = [tile[b, s, k].astype(F32) for k in range(4)]
                for c in range(4):
                    total = jnp.zeros((128, 128), F32)
                    for k in range(4):
                        total = total + jnp.where(pick[b, s, k] == c, parts[k], 0.0)
                    out[d, s, b * 128 : (b + 1) * 128, c * 128 : (c + 1) * 128] = total.astype(BF)


def source_of(back):
    zl, zh, core = lax.axis_index("zl"), lax.axis_index("zh"), lax.axis_index("core")
    turn = jnp.int32(0)
    for i in range(2):
        for j in range(4):
            for k in range(2):
                here = jnp.logical_and(jnp.logical_and(zl == i, zh == j), core == k)
                turn = jnp.where(here, TURN[i][j][k], turn)
    return lax.rem(lax.axis_index("y") - lax.axis_index("x") + turn + 8 - back, 4)


def terms(d, mix, keys, parts):
    total = None
    for (back, half), part in zip(keys, parts):
        left = mix[d, source_of(back), :, half * 256 : (half + 1) * 256]
        term = jnp.dot(left, part[...], preferred_element_type=F32)
        total = term if total is None else total + term
    return total


def first_kernel(keys, mix, *refs):
    for d in range(2):
        refs[-1][d] = terms(d, mix, keys, refs[:-1])


def next_kernel(keys, mix, begun, *refs):
    for d in range(2):
        refs[-1][d] = begun[d] + terms(d, mix, keys, refs[:-1])


def last_kernel(keys, mix, begun, *refs):
    core = lax.axis_index("core")
    for d, at in enumerate((core, 1 - core)):
        total = (begun[d] + terms(d, mix, keys, refs[:-1])).astype(BF)
        for r in range(8):
            refs[-1][r, at] = total[r * 64 : (r + 1) * 64]


def rows_kernel(recv, out):
    total = recv[0].astype(F32)
    for r in range(1, 8):
        total = total + recv[r].astype(F32)
    out[...] = total.astype(BF)


def with_bias(block, row):
    high = row.astype(BF).astype(F32)
    low = row - high
    at = lax.broadcasted_iota(jnp.int32, (8, 384), 0)
    extra = jnp.where(at == 0, high, jnp.where(at == 1, low, 0.0))
    return jnp.concatenate([block, extra], axis=0).astype(BF)


def layer_kernel(mine, other, weight, bias, cot, other_cot, out, packed):
    first = lax.axis_index("core") == 0
    left = jnp.where(first, mine[...], other[...]).reshape(128, 384)
    right = jnp.where(first, other[...], mine[...]).reshape(128, 384)
    mixed = jnp.concatenate([left, right], axis=1)
    pre = jnp.dot(mixed, weight[...], preferred_element_type=F32) + bias[...]
    sig = jax.nn.sigmoid(pre)
    act = pre * sig
    out[...] = jnp.where(first, act[:64], act[64:]).astype(BF)
    both = jnp.concatenate(
        [jnp.where(first, cot[...], other_cot[...]), jnp.where(first, other_cot[...], cot[...])], axis=0
    )
    grad = both.astype(F32) * sig * (1.0 + pre * (1.0 - sig))
    low = jnp.where(first, grad[:, :384], grad[:, 384:]).astype(BF)
    block = lax.dot_general(mixed, low, (((0,), (0,)), ((), ())), preferred_element_type=F32)
    row = jnp.sum(low.astype(F32), axis=0, keepdims=True)
    for i in range(16):
        packed[i] = with_bias(block[i * 48 : (i + 1) * 48], row)


def resplit(total):
    return with_bias(total[:48], total[48:49] + total[49:50])


def plane_kernel(recv, out):
    total = recv[0].astype(F32)
    for r in range(1, 16):
        total = total + recv[r].astype(F32)
    out[...] = resplit(total)


def pair_kernel(one, two, out):
    out[...] = resplit(one[...].astype(F32) + two[...].astype(F32))


def four_kernel(copies, one, two, three, four, out):
    total = (one[...].astype(F32) + two[...].astype(F32)) + (three[...].astype(F32) + four[...].astype(F32))
    value = resplit(total)
    for i in range(copies):
        out[i] = value


def write_columns(source, at, grad, rows, sems):
    start = pl.multiple_of(at * 384, 384)
    copies = []
    for i in range(4):
        for j in range(4):
            rows[i, j * 48 : (j + 1) * 48] = source[i * 4 + j].astype(F32)[:48]
        copies.append(
            pltpu.make_async_copy(rows.at[i], grad.at[pl.ds(i * 192, 192), pl.ds(start, 384)], sems.at[i])
        )
        copies[-1].start()
    return copies


def own_half_kernel(own, grad, rows, sems):
    for copy in write_columns(own, lax.axis_index("core"), grad, rows, sems):
        copy.wait()


def other_half_kernel(own, other, begun, grad, bias, rows, sems, row, row_sem):
    del begun
    first = lax.axis_index("core") == 0
    mine, theirs = own[0].astype(F32), other[0].astype(F32)
    mine = mine[48:49] + mine[49:50]
    theirs = theirs[48:49] + theirs[49:50]
    both = jnp.concatenate([jnp.where(first, mine, theirs), jnp.where(first, theirs, mine)], axis=1)
    row[...] = both.reshape(768)
    copies = [pltpu.make_async_copy(row, bias, row_sem)]
    copies[0].start()
    copies += write_columns(other, 1 - lax.axis_index("core"), grad, rows, sems)
    for copy in copies:
        copy.wait()


def neighbours(piece, step):
    return [lax.ppermute(piece, "zh", shift(4, step))] + [lax.ppermute(piece, "y", shift(4, k)) for k in BACK[1:]]


def product(kernel, keys, mix, parts, begun=None):
    last = kernel is last_kernel
    extra = [] if begun is None else [begun]
    return call(
        lambda *refs: kernel(keys, *refs),
        struct((8, 2, 64, 384), BF) if last else struct((2, 512, 384), F32),
        [vmem()] * (1 + len(extra) + len(parts)),
        vmem(),
        aliases={1: 0} if extra and not last else None,
        flops=4 * 512 * 256 * 384 * len(parts),
    )(mix, *extra, *parts)


def on_device(features, tiles, tile_cols, tile_mask, weight, bias, cotangent):
    with jax.named_scope("spread_features"):
        halves = call(
            pick_kernel,
            (struct((256, 384), BF), struct((256, 384), BF)),
            [hbm()],
            (vmem(), vmem()),
            [pltpu.SemaphoreType.DMA((2,))],
        )(features)
        *halves, tiles, tile_cols, tile_mask = lax.optimization_barrier((*halves, tiles, tile_cols, tile_mask))
        own = [lax.ppermute(half, AXES, first_hop()) for half in halves]
    with jax.named_scope("spread_tiles"):
        picks = jnp.where(tile_mask != 0, tile_cols, -1)
        there = [lax.ppermute(value, "core", shift(2, 1)) for value in (picks, tiles)]
        mix = call(
            spread_kernel,
            struct((2, 4, 512, 512), BF),
            [smem(), smem(), vmem(), vmem()],
            vmem(),
        )(picks, there[0], tiles, there[1])
    own[0], mix = lax.optimization_barrier((own[0], mix))
    with jax.named_scope("spread_features"):
        early = neighbours(own[0], 3)
    with jax.named_scope("spread_features"):
        late = neighbours(own[1], 1)
    with jax.named_scope("aggregate"):
        begun = product(first_kernel, [(0, 0), (0, 1)], mix, own)
        begun = product(next_kernel, [(back, 0) for back in BACK], mix, early, begun)
        other_cot = lax.ppermute(cotangent, "core", shift(2, 1))
        begun, other_cot = lax.optimization_barrier((begun, other_cot))
        begun = product(next_kernel, [(BACK[0], 1)], mix, late[:1], begun)
        begun = product(next_kernel, [(BACK[1], 1)], mix, late[1:2], begun)
        partial = product(last_kernel, [(BACK[2], 1)], mix, late[2:], begun)
    with jax.named_scope("sum_over_rep"):
        recv = lax.all_to_all(partial, REP, 0, 0, tiled=True)
        mixed = call(rows_kernel, struct((2, 64, 384), BF), [vmem()], vmem())(recv)
        other_mixed = lax.ppermute(mixed, "core", shift(2, 1))
    with jax.named_scope("layer"):
        output, packed = call(
            layer_kernel,
            (struct((64, 768), BF), struct((16, 56, 384), BF)),
            [vmem()] * 6,
            (vmem(), vmem()),
        )(mixed, other_mixed, weight, bias.reshape(1, 768), cotangent, other_cot)
    with jax.named_scope("sum_over_plane"):
        recv = lax.all_to_all(packed.reshape(896, 384), PLANE, 0, 0, tiled=True)
        part = call(plane_kernel, struct((56, 384), BF), [vmem()], vmem())(recv.reshape(16, 56, 384))
    with jax.named_scope("sum_over_z"):
        beside = lax.ppermute(part, "zl", shift(2, 1))
        part = call(pair_kernel, struct((56, 384), BF), [vmem()] * 2, vmem())(part, beside)
        chain = [lax.ppermute(part, "zh", shift(4, back)) for back in BACK]
        whole = call(
            lambda *refs: four_kernel(16, *refs), struct((16, 56, 384), BF), [vmem()] * 4, vmem()
        )(part, *chain)
    with jax.named_scope("gather_plane"):
        mine = lax.all_to_all(whole.reshape(896, 384), PLANE, 0, 0, tiled=True)
        theirs = lax.ppermute(mine, "core", shift(2, 1)).reshape(16, 56, 384)
        mine = mine.reshape(16, 56, 384)
    with jax.named_scope("finish"):
        scratch = [pltpu.VMEM((4, 192, 384), F32), pltpu.SemaphoreType.DMA((4,))]
        grad = call(own_half_kernel, struct((768, 768), F32), [vmem()], anyspace(), scratch)(mine)
        grad_weight, grad_bias = call(
            other_half_kernel,
            (struct((768, 768), F32), struct((768,), F32)),
            [vmem(), vmem(), anyspace()],
            (anyspace(), hbm()),
            scratch + [pltpu.VMEM((768,), F32), pltpu.SemaphoreType.DMA],
            aliases={2: 0},
        )(mine, theirs, grad)
    return output, grad_weight, grad_bias


def solution(mesh):
    fine = Mesh(mesh.devices.reshape(SIZES), AXES)
    placed = (
        P(DOM, None),
        P(DOM, REP, None, None, None),
        P(DOM, REP, None),
        P(DOM, REP, None),
        P(),
        P(),
        P(DOM + REP, None),
    )
    return jax.shard_map(
        on_device,
        mesh=fine,
        in_specs=placed,
        out_specs=(P(DOM + REP, None), P(), P()),
        check_vma=False,
    )
```

```python
import jax
import jax.numpy as jnp
import numpy as np
from jax import lax
from jax.experimental import pallas as pl
from jax.experimental.pallas import tpu as pltpu
from jax.sharding import Mesh, PartitionSpec as P

AXES = ("y", "zh", "core", "x", "zl")
SIZES = (4, 4, 2, 4, 2)
DOM = ("y", "zh", "core")
REP = ("x", "zl")
PLANE = ("x", "y")
BF = jnp.bfloat16
F32 = jnp.float32
BACK = (2, 1, 3)
NEAR = (1, 3, 2)
VMEM_LIMIT = 32 * 1024 * 1024

TURN = (((1, 0), (3, 2), (1, 0), (3, 2)), ((2, 0), (0, 2), (2, 0), (0, 2)))
OFFSET = (
    ((3, 2, 0, 1), (2, 0, 1, 3), (0, 2, 3, 1), (1, 3, 2, 0), (2, 0, 1, 3), (0, 1, 3, 2), (1, 3, 0, 2), (3, 1, 2, 0)),
    ((3, 2, 0, 1), (2, 1, 3, 0), (1, 2, 0, 3), (3, 0, 2, 1), (1, 0, 2, 3), (3, 1, 0, 2), (1, 3, 2, 0), (0, 3, 1, 2)),
)


def first_hop():
    pairs = []
    for target in np.ndindex(*SIZES):
        y, zh, core, x, zl = target
        s = (y - x + TURN[zl][zh][core]) % 4
        source = (x, 2 * zl + s // 2, s % 2, (x + OFFSET[zl][2 * s + core][zh]) % 4, core)
        pairs.append((int(np.ravel_multi_index(source, SIZES)), int(np.ravel_multi_index(target, SIZES))))
    return sorted(pairs)


def shift(n, k):
    return [(i, (i + k) % n) for i in range(n)]


def vmem():
    return pl.BlockSpec(memory_space=pltpu.VMEM)


def smem():
    return pl.BlockSpec(memory_space=pltpu.SMEM)


def hbm():
    return pl.BlockSpec(memory_space=pltpu.HBM)


def anyspace():
    return pl.BlockSpec(memory_space=pl.ANY)


def struct(shape, dtype):
    return jax.ShapeDtypeStruct(shape, dtype)


def call(kernel, shapes, specs, out_specs, scratch=(), aliases=None, flops=0):
    return pl.pallas_call(
        kernel,
        out_shape=shapes,
        in_specs=specs,
        out_specs=out_specs,
        scratch_shapes=scratch,
        input_output_aliases=aliases or {},
        compiler_params=pltpu.CompilerParams(vmem_limit_bytes=VMEM_LIMIT),
        cost_estimate=pl.CostEstimate(flops=flops, bytes_accessed=1 << 20, transcendentals=0),
    )


def pick_kernel(features, one, two, sems):
    start = pl.multiple_of(lax.axis_index("zl") * 384, 384)
    copies = [
        pltpu.make_async_copy(features.at[pl.ds(i * 256, 256), pl.ds(start, 384)], out, sems.at[i])
        for i, out in enumerate((one, two))
    ]
    for copy in copies:
        copy.start()
    for copy in copies:
        copy.wait()


def spread_kernel(picks, other_picks, tiles, other_tiles, out):
    for d, (pick, tile) in enumerate(((picks, tiles), (other_picks, other_tiles))):
        for b in range(4):
            for s in range(4):
                parts = [tile[b, s, k].astype(F32) for k in range(4)]
                for c in range(4):
                    total = jnp.zeros((128, 128), F32)
                    for k in range(4):
                        total = total + jnp.where(pick[b, s, k] == c, parts[k], 0.0)
                    out[d, s, b * 128 : (b + 1) * 128, c * 128 : (c + 1) * 128] = total.astype(BF)


def source_of(back):
    zl, zh, core = lax.axis_index("zl"), lax.axis_index("zh"), lax.axis_index("core")
    turn = jnp.int32(0)
    for i in range(2):
        for j in range(4):
            for k in range(2):
                here = jnp.logical_and(jnp.logical_and(zl == i, zh == j), core == k)
                turn = jnp.where(here, TURN[i][j][k], turn)
    return lax.rem(lax.axis_index("y") - lax.axis_index("x") + turn + 8 - back, 4)


def terms(d, mix, keys, parts):
    total = None
    for (back, half), part in zip(keys, parts):
        left = mix[d, source_of(back), :, half * 256 : (half + 1) * 256]
        term = jnp.dot(left, part[...], preferred_element_type=F32)
        total = term if total is None else total + term
    return total


def first_kernel(keys, mix, *refs):
    for d in range(2):
        refs[-1][d] = terms(d, mix, keys, refs[:-1])


def next_kernel(keys, mix, begun, *refs):
    for d in range(2):
        refs[-1][d] = begun[d] + terms(d, mix, keys, refs[:-1])


def last_kernel(keys, mix, begun, *refs):
    core = lax.axis_index("core")
    for d, at in enumerate((core, 1 - core)):
        total = (begun[d] + terms(d, mix, keys, refs[:-1])).astype(BF)
        for r in range(8):
            refs[-1][r, at] = total[r * 64 : (r + 1) * 64]


def rows_kernel(recv, out):
    total = recv[0].astype(F32)
    for r in range(1, 8):
        total = total + recv[r].astype(F32)
    out[...] = total.astype(BF)


def with_bias(block, row):
    high = row.astype(BF).astype(F32)
    low = row - high
    at = lax.broadcasted_iota(jnp.int32, (8, 384), 0)
    extra = jnp.where(at == 0, high, jnp.where(at == 1, low, 0.0))
    return jnp.concatenate([block, extra], axis=0).astype(BF)


def layer_kernel(mine, other, weight, bias, cot, other_cot, out, packed):
    first = lax.axis_index("core") == 0
    left = jnp.where(first, mine[...], other[...]).reshape(128, 384)
    right = jnp.where(first, other[...], mine[...]).reshape(128, 384)
    mixed = jnp.concatenate([left, right], axis=1)
    pre = jnp.dot(mixed, weight[...], preferred_element_type=F32) + bias[...]
    sig = jax.nn.sigmoid(pre)
    act = pre * sig
    out[...] = jnp.where(first, act[:64], act[64:]).astype(BF)
    both = jnp.concatenate(
        [jnp.where(first, cot[...], other_cot[...]), jnp.where(first, other_cot[...], cot[...])], axis=0
    )
    grad = both.astype(F32) * sig * (1.0 + pre * (1.0 - sig))
    low = jnp.where(first, grad[:, :384], grad[:, 384:]).astype(BF)
    block = lax.dot_general(mixed, low, (((0,), (0,)), ((), ())), preferred_element_type=F32)
    row = jnp.sum(low.astype(F32), axis=0, keepdims=True)
    for i in range(16):
        packed[i] = with_bias(block[i * 48 : (i + 1) * 48], row)


def resplit(total):
    return with_bias(total[:48], total[48:49] + total[49:50])


def plane_kernel(recv, out):
    total = recv[0].astype(F32)
    for r in range(1, 16):
        total = total + recv[r].astype(F32)
    out[...] = resplit(total)


def pair_kernel(one, two, out):
    out[...] = resplit(one[...].astype(F32) + two[...].astype(F32))


def four_kernel(copies, one, two, three, four, out):
    total = (one[...].astype(F32) + two[...].astype(F32)) + (three[...].astype(F32) + four[...].astype(F32))
    value = resplit(total)
    for i in range(copies):
        out[i] = value


def write_columns(source, at, grad, rows, sems):
    start = pl.multiple_of(at * 384, 384)
    copies = []
    for i in range(4):
        for j in range(4):
            rows[i, j * 48 : (j + 1) * 48] = source[i * 4 + j].astype(F32)[:48]
        copies.append(
            pltpu.make_async_copy(rows.at[i], grad.at[pl.ds(i * 192, 192), pl.ds(start, 384)], sems.at[i])
        )
        copies[-1].start()
    return copies


def own_half_kernel(own, grad, rows, sems):
    for copy in write_columns(own, lax.axis_index("core"), grad, rows, sems):
        copy.wait()


def other_half_kernel(own, other, begun, grad, bias, rows, sems, row, row_sem):
    del begun
    first = lax.axis_index("core") == 0
    mine, theirs = own[0].astype(F32), other[0].astype(F32)
    mine = mine[48:49] + mine[49:50]
    theirs = theirs[48:49] + theirs[49:50]
    both = jnp.concatenate([jnp.where(first, mine, theirs), jnp.where(first, theirs, mine)], axis=1)
    row[...] = both.reshape(768)
    copies = [pltpu.make_async_copy(row, bias, row_sem)]
    copies[0].start()
    copies += write_columns(other, 1 - lax.axis_index("core"), grad, rows, sems)
    for copy in copies:
        copy.wait()


def neighbours(piece, order, step):
    return [
        lax.ppermute(piece, "zh", shift(4, step)) if back == 2 else lax.ppermute(piece, "y", shift(4, back))
        for back in order
    ]


def product(kernel, keys, mix, parts, begun=None):
    last = kernel is last_kernel
    extra = [] if begun is None else [begun]
    return call(
        lambda *refs: kernel(keys, *refs),
        struct((8, 2, 64, 384), BF) if last else struct((2, 512, 384), F32),
        [vmem()] * (1 + len(extra) + len(parts)),
        vmem(),
        aliases={1: 0} if extra and not last else None,
        flops=4 * 512 * 256 * 384 * len(parts),
    )(mix, *extra, *parts)


def on_device(features, tiles, tile_cols, tile_mask, weight, bias, cotangent):
    with jax.named_scope("spread_features"):
        halves = call(
            pick_kernel,
            (struct((256, 384), BF), struct((256, 384), BF)),
            [hbm()],
            (vmem(), vmem()),
            [pltpu.SemaphoreType.DMA((2,))],
        )(features)
        *halves, tiles, tile_cols, tile_mask = lax.optimization_barrier((*halves, tiles, tile_cols, tile_mask))
        own = [lax.ppermute(half, AXES, first_hop()) for half in halves]
    with jax.named_scope("spread_tiles"):
        picks = jnp.where(tile_mask != 0, tile_cols, -1)
        there = [lax.ppermute(value, "core", shift(2, 1)) for value in (picks, tiles)]
        mix = call(
            spread_kernel,
            struct((2, 4, 512, 512), BF),
            [smem(), smem(), vmem(), vmem()],
            vmem(),
        )(picks, there[0], tiles, there[1])
    own[0], mix = lax.optimization_barrier((own[0], mix))
    with jax.named_scope("spread_features"):
        early = neighbours(own[0], NEAR, 3)
    with jax.named_scope("spread_features"):
        late = neighbours(own[1], BACK, 1)
    with jax.named_scope("aggregate"):
        begun = product(first_kernel, [(0, 0), (0, 1)], mix, own)
        begun = product(next_kernel, [(back, 0) for back in NEAR], mix, early, begun)
        other_cot = lax.ppermute(cotangent, "core", shift(2, 1))
        begun, other_cot = lax.optimization_barrier((begun, other_cot))
        begun = product(next_kernel, [(BACK[0], 1)], mix, late[:1], begun)
        begun = product(next_kernel, [(BACK[1], 1)], mix, late[1:2], begun)
        partial = product(last_kernel, [(BACK[2], 1)], mix, late[2:], begun)
    with jax.named_scope("sum_over_rep"):
        recv = lax.all_to_all(partial, REP, 0, 0, tiled=True)
        mixed = call(rows_kernel, struct((2, 64, 384), BF), [vmem()], vmem())(recv)
        other_mixed = lax.ppermute(mixed, "core", shift(2, 1))
    with jax.named_scope("layer"):
        output, packed = call(
            layer_kernel,
            (struct((64, 768), BF), struct((16, 56, 384), BF)),
            [vmem()] * 6,
            (vmem(), vmem()),
        )(mixed, other_mixed, weight, bias.reshape(1, 768), cotangent, other_cot)
    with jax.named_scope("sum_over_plane"):
        recv = lax.all_to_all(packed.reshape(896, 384), PLANE, 0, 0, tiled=True)
        part = call(plane_kernel, struct((56, 384), BF), [vmem()], vmem())(recv.reshape(16, 56, 384))
    with jax.named_scope("sum_over_z"):
        beside = lax.ppermute(part, "zl", shift(2, 1))
        part = call(pair_kernel, struct((56, 384), BF), [vmem()] * 2, vmem())(part, beside)
        chain = [lax.ppermute(part, "zh", shift(4, back)) for back in BACK]
        whole = call(
            lambda *refs: four_kernel(16, *refs), struct((16, 56, 384), BF), [vmem()] * 4, vmem()
        )(part, *chain)
    with jax.named_scope("gather_plane"):
        mine = lax.all_to_all(whole.reshape(896, 384), PLANE, 0, 0, tiled=True)
        theirs = lax.ppermute(mine, "core", shift(2, 1)).reshape(16, 56, 384)
        mine = mine.reshape(16, 56, 384)
    with jax.named_scope("finish"):
        scratch = [pltpu.VMEM((4, 192, 384), F32), pltpu.SemaphoreType.DMA((4,))]
        grad = call(own_half_kernel, struct((768, 768), F32), [vmem()], anyspace(), scratch)(mine)
        grad_weight, grad_bias = call(
            other_half_kernel,
            (struct((768, 768), F32), struct((768,), F32)),
            [vmem(), vmem(), anyspace()],
            (anyspace(), hbm()),
            scratch + [pltpu.VMEM((768,), F32), pltpu.SemaphoreType.DMA],
            aliases={2: 0},
        )(mine, theirs, grad)
    return output, grad_weight, grad_bias


def solution(mesh):
    fine = Mesh(mesh.devices.reshape(SIZES), AXES)
    placed = (
        P(DOM, None),
        P(DOM, REP, None, None, None),
        P(DOM, REP, None),
        P(DOM, REP, None),
        P(),
        P(),
        P(DOM + REP, None),
    )
    return jax.shard_map(
        on_device,
        mesh=fine,
        in_specs=placed,
        out_specs=(P(DOM + REP, None), P(), P()),
        check_vma=False,
    )
```

```python
import jax
import jax.numpy as jnp
import numpy as np
from jax import lax
from jax.experimental import pallas as pl
from jax.experimental.pallas import tpu as pltpu
from jax.sharding import Mesh, PartitionSpec as P

AXES = ("y", "zh", "core", "x", "zl")
SIZES = (4, 4, 2, 4, 2)
DOM = ("y", "zh", "core")
REP = ("x", "zl")
PLANE = ("x", "y")
BF = jnp.bfloat16
F32 = jnp.float32
BACK = (2, 1, 3)
NEAR = (1, 3, 2)
VMEM_LIMIT = 32 * 1024 * 1024

TURN = (((1, 0), (3, 2), (1, 0), (3, 2)), ((2, 0), (0, 2), (2, 0), (0, 2)))
OFFSET = (
    ((3, 2, 0, 1), (2, 0, 1, 3), (0, 2, 3, 1), (1, 3, 2, 0), (2, 0, 1, 3), (0, 1, 3, 2), (1, 3, 0, 2), (3, 1, 2, 0)),
    ((3, 2, 0, 1), (2, 1, 3, 0), (1, 2, 0, 3), (3, 0, 2, 1), (1, 0, 2, 3), (3, 1, 0, 2), (1, 3, 2, 0), (0, 3, 1, 2)),
)


def first_hop():
    pairs = []
    for target in np.ndindex(*SIZES):
        y, zh, core, x, zl = target
        s = (y - x + TURN[zl][zh][core]) % 4
        source = (x, 2 * zl + s // 2, s % 2, (x + OFFSET[zl][2 * s + core][zh]) % 4, core)
        pairs.append((int(np.ravel_multi_index(source, SIZES)), int(np.ravel_multi_index(target, SIZES))))
    return sorted(pairs)


def shift(n, k):
    return [(i, (i + k) % n) for i in range(n)]


def vmem():
    return pl.BlockSpec(memory_space=pltpu.VMEM)


def smem():
    return pl.BlockSpec(memory_space=pltpu.SMEM)


def hbm():
    return pl.BlockSpec(memory_space=pltpu.HBM)


def anyspace():
    return pl.BlockSpec(memory_space=pl.ANY)


def struct(shape, dtype):
    return jax.ShapeDtypeStruct(shape, dtype)


def call(kernel, shapes, specs, out_specs, scratch=(), aliases=None, flops=0):
    return pl.pallas_call(
        kernel,
        out_shape=shapes,
        in_specs=specs,
        out_specs=out_specs,
        scratch_shapes=scratch,
        input_output_aliases=aliases or {},
        compiler_params=pltpu.CompilerParams(vmem_limit_bytes=VMEM_LIMIT),
        cost_estimate=pl.CostEstimate(flops=flops, bytes_accessed=1 << 20, transcendentals=0),
    )


def pick_kernel(features, one, two, sems):
    start = pl.multiple_of(lax.axis_index("zl") * 384, 384)
    copies = [
        pltpu.make_async_copy(features.at[pl.ds(i * 256, 256), pl.ds(start, 384)], out, sems.at[i])
        for i, out in enumerate((one, two))
    ]
    for copy in copies:
        copy.start()
    for copy in copies:
        copy.wait()


def spread_kernel(picks, other_picks, tiles, other_tiles, out):
    for d, (pick, tile) in enumerate(((picks, tiles), (other_picks, other_tiles))):
        for b in range(4):
            for s in range(4):
                parts = [tile[b, s, k].astype(F32) for k in range(4)]
                for c in range(4):
                    total = jnp.zeros((128, 128), F32)
                    for k in range(4):
                        total = total + jnp.where(pick[b, s, k] == c, parts[k], 0.0)
                    out[d, s, b * 128 : (b + 1) * 128, c * 128 : (c + 1) * 128] = total.astype(BF)


def source_of(back):
    zl, zh, core = lax.axis_index("zl"), lax.axis_index("zh"), lax.axis_index("core")
    turn = jnp.int32(0)
    for i in range(2):
        for j in range(4):
            for k in range(2):
                here = jnp.logical_and(jnp.logical_and(zl == i, zh == j), core == k)
                turn = jnp.where(here, TURN[i][j][k], turn)
    return lax.rem(lax.axis_index("y") - lax.axis_index("x") + turn + 8 - back, 4)


def terms(d, mix, keys, parts):
    total = None
    for (back, half), part in zip(keys, parts):
        left = mix[d, source_of(back), :, half * 256 : (half + 1) * 256]
        term = jnp.dot(left, part[...], preferred_element_type=F32)
        total = term if total is None else total + term
    return total


def first_kernel(keys, mix, *refs):
    for d in range(2):
        refs[-1][d] = terms(d, mix, keys, refs[:-1])


def next_kernel(keys, mix, begun, *refs):
    for d in range(2):
        refs[-1][d] = begun[d] + terms(d, mix, keys, refs[:-1])


def last_kernel(keys, mix, begun, *refs):
    core = lax.axis_index("core")
    for d, at in enumerate((core, 1 - core)):
        total = (begun[d] + terms(d, mix, keys, refs[:-1])).astype(BF)
        for r in range(8):
            refs[-1][r, at] = total[r * 64 : (r + 1) * 64]


def rows_kernel(recv, out):
    total = recv[0].astype(F32)
    for r in range(1, 8):
        total = total + recv[r].astype(F32)
    out[...] = total.astype(BF)


def with_bias(block, row):
    high = row.astype(BF).astype(F32)
    low = row - high
    at = lax.broadcasted_iota(jnp.int32, (8, 384), 0)
    extra = jnp.where(at == 0, high, jnp.where(at == 1, low, 0.0))
    return jnp.concatenate([block, extra], axis=0).astype(BF)


def layer_kernel(mine, other, weight, bias, cot, other_cot, out, packed):
    first = lax.axis_index("core") == 0
    left = jnp.where(first, mine[...], other[...]).reshape(128, 384)
    right = jnp.where(first, other[...], mine[...]).reshape(128, 384)
    mixed = jnp.concatenate([left, right], axis=1)
    pre = jnp.dot(mixed, weight[...], preferred_element_type=F32) + bias[...]
    sig = jax.nn.sigmoid(pre)
    act = pre * sig
    out[...] = jnp.where(first, act[:64], act[64:]).astype(BF)
    both = jnp.concatenate(
        [jnp.where(first, cot[...], other_cot[...]), jnp.where(first, other_cot[...], cot[...])], axis=0
    )
    grad = both.astype(F32) * sig * (1.0 + pre * (1.0 - sig))
    low = jnp.where(first, grad[:, :384], grad[:, 384:]).astype(BF)
    block = lax.dot_general(mixed, low, (((0,), (0,)), ((), ())), preferred_element_type=F32)
    row = jnp.sum(low.astype(F32), axis=0, keepdims=True)
    for i in range(16):
        packed[i] = with_bias(block[i * 48 : (i + 1) * 48], row)


def resplit(total):
    return with_bias(total[:48], total[48:49] + total[49:50])


def plane_kernel(recv, out):
    total = recv[0].astype(F32)
    for r in range(1, 16):
        total = total + recv[r].astype(F32)
    out[...] = resplit(total)


def pair_kernel(one, two, out):
    out[...] = resplit(one[...].astype(F32) + two[...].astype(F32))


def four_kernel(copies, own, back, ahead, across, out):
    total = (own[...].astype(F32) + across[...].astype(F32)) + (back[...].astype(F32) + ahead[...].astype(F32))
    value = resplit(total)
    for i in range(copies):
        out[i] = value


def write_columns(source, at, grad, rows, sems):
    start = pl.multiple_of(at * 384, 384)
    copies = []
    for i in range(4):
        for j in range(4):
            rows[i, j * 48 : (j + 1) * 48] = source[i * 4 + j].astype(F32)[:48]
        copies.append(
            pltpu.make_async_copy(rows.at[i], grad.at[pl.ds(i * 192, 192), pl.ds(start, 384)], sems.at[i])
        )
        copies[-1].start()
    return copies


def own_half_kernel(own, grad, rows, sems):
    for copy in write_columns(own, lax.axis_index("core"), grad, rows, sems):
        copy.wait()


def other_half_kernel(own, other, begun, grad, bias, rows, sems, row, row_sem):
    del begun
    first = lax.axis_index("core") == 0
    mine, theirs = own[0].astype(F32), other[0].astype(F32)
    mine = mine[48:49] + mine[49:50]
    theirs = theirs[48:49] + theirs[49:50]
    both = jnp.concatenate([jnp.where(first, mine, theirs), jnp.where(first, theirs, mine)], axis=1)
    row[...] = both.reshape(768)
    copies = [pltpu.make_async_copy(row, bias, row_sem)]
    copies[0].start()
    copies += write_columns(other, 1 - lax.axis_index("core"), grad, rows, sems)
    for copy in copies:
        copy.wait()


def neighbours(piece, order, step):
    return [
        lax.ppermute(piece, "zh", shift(4, step)) if back == 2 else lax.ppermute(piece, "y", shift(4, back))
        for back in order
    ]


def product(kernel, keys, mix, parts, begun=None):
    last = kernel is last_kernel
    extra = [] if begun is None else [begun]
    return call(
        lambda *refs: kernel(keys, *refs),
        struct((8, 2, 64, 384), BF) if last else struct((2, 512, 384), F32),
        [vmem()] * (1 + len(extra) + len(parts)),
        vmem(),
        aliases={1: 0} if extra and not last else None,
        flops=4 * 512 * 256 * 384 * len(parts),
    )(mix, *extra, *parts)


def on_device(features, tiles, tile_cols, tile_mask, weight, bias, cotangent):
    with jax.named_scope("spread_features"):
        halves = call(
            pick_kernel,
            (struct((256, 384), BF), struct((256, 384), BF)),
            [hbm()],
            (vmem(), vmem()),
            [pltpu.SemaphoreType.DMA((2,))],
        )(features)
        *halves, tiles, tile_cols, tile_mask = lax.optimization_barrier((*halves, tiles, tile_cols, tile_mask))
        own = [lax.ppermute(half, AXES, first_hop()) for half in halves]
    with jax.named_scope("spread_tiles"):
        picks = jnp.where(tile_mask != 0, tile_cols, -1)
        there = [lax.ppermute(value, "core", shift(2, 1)) for value in (picks, tiles)]
        mix = call(
            spread_kernel,
            struct((2, 4, 512, 512), BF),
            [smem(), smem(), vmem(), vmem()],
            vmem(),
        )(picks, there[0], tiles, there[1])
    own[0], mix = lax.optimization_barrier((own[0], mix))
    with jax.named_scope("spread_features"):
        early = neighbours(own[0], NEAR, 3)
    with jax.named_scope("spread_features"):
        late = neighbours(own[1], BACK, 1)
    with jax.named_scope("aggregate"):
        begun = product(first_kernel, [(0, 0), (0, 1)], mix, own)
        begun = product(next_kernel, [(back, 0) for back in NEAR], mix, early, begun)
        other_cot = lax.ppermute(cotangent, "core", shift(2, 1))
        begun, other_cot = lax.optimization_barrier((begun, other_cot))
        begun = product(next_kernel, [(BACK[0], 1)], mix, late[:1], begun)
        partial = product(last_kernel, [(back, 1) for back in BACK[1:]], mix, late[1:], begun)
    with jax.named_scope("sum_over_rep"):
        recv = lax.all_to_all(partial, REP, 0, 0, tiled=True)
        mixed = call(rows_kernel, struct((2, 64, 384), BF), [vmem()], vmem())(recv)
        other_mixed = lax.ppermute(mixed, "core", shift(2, 1))
    with jax.named_scope("layer"):
        output, packed = call(
            layer_kernel,
            (struct((64, 768), BF), struct((16, 56, 384), BF)),
            [vmem()] * 6,
            (vmem(), vmem()),
        )(mixed, other_mixed, weight, bias.reshape(1, 768), cotangent, other_cot)
    with jax.named_scope("sum_over_plane"):
        recv = lax.all_to_all(packed.reshape(896, 384), PLANE, 0, 0, tiled=True)
        part = call(plane_kernel, struct((56, 384), BF), [vmem()], vmem())(recv.reshape(16, 56, 384))
    with jax.named_scope("sum_over_z"):
        beside = lax.ppermute(part, "zl", shift(2, 1))
        part = call(pair_kernel, struct((56, 384), BF), [vmem()] * 2, vmem())(part, beside)
        chain = [lax.ppermute(part, "zh", shift(4, back)) for back in NEAR]
        whole = call(
            lambda *refs: four_kernel(16, *refs), struct((16, 56, 384), BF), [vmem()] * 4, vmem()
        )(part, *chain)
    with jax.named_scope("gather_plane"):
        mine = lax.all_to_all(whole.reshape(896, 384), PLANE, 0, 0, tiled=True)
        theirs = lax.ppermute(mine, "core", shift(2, 1)).reshape(16, 56, 384)
        mine = mine.reshape(16, 56, 384)
    with jax.named_scope("finish"):
        scratch = [pltpu.VMEM((4, 192, 384), F32), pltpu.SemaphoreType.DMA((4,))]
        grad = call(own_half_kernel, struct((768, 768), F32), [vmem()], anyspace(), scratch)(mine)
        grad_weight, grad_bias = call(
            other_half_kernel,
            (struct((768, 768), F32), struct((768,), F32)),
            [vmem(), vmem(), anyspace()],
            (anyspace(), hbm()),
            scratch + [pltpu.VMEM((768,), F32), pltpu.SemaphoreType.DMA],
            aliases={2: 0},
        )(mine, theirs, grad)
    return output, grad_weight, grad_bias


def solution(mesh):
    fine = Mesh(mesh.devices.reshape(SIZES), AXES)
    placed = (
        P(DOM, None),
        P(DOM, REP, None, None, None),
        P(DOM, REP, None),
        P(DOM, REP, None),
        P(),
        P(),
        P(DOM + REP, None),
    )
    return jax.shard_map(
        on_device,
        mesh=fine,
        in_specs=placed,
        out_specs=(P(DOM + REP, None), P(), P()),
        check_vma=False,
    )
```
